128 devices in a mesh: lon: 32 (over z_lo, y, x), lat: 4 (over z_hi, core).
Axes of the slice: x: 4, y: 4, z: 4 (z_hi: 2, z_lo: 2; z = z_hi * 2 + z_lo), core: 2. Of those that a mesh axis runs over, the one named last changes fastest.
Arguments:
- kernels: float32 [72, 1048576], P(None, ('lon', 'lat')), may hold values from 0.2 to 2
- weighted_residuals: float32 [1048576], P(('lon', 'lat')), may hold values from -6 to 6
- sounding_columns: int32 [1048576], P(('lon', 'lat')), may hold values from 0 to 6143
- segment_counts: int32 [128, 128], P(('lon', 'lat')), may hold values from 0 to 64, as said below
- courant: float32 [2, 72, 1536, 512], P(None, None, 'lon', 'lat'), may hold values from -0.48 to 0.48
- mix_strength: float32 [1536, 512], P('lon', 'lat'), may hold values from 0.05 to 0.6
- cloud_top: int32 [1536, 512], P('lon', 'lat'), may hold values from 1 to 72
- redistribution: float32 [72, 72], replicated, may hold values from -0.75 to 0.75
Outputs:
- sensitivity: float32 [72, 1536, 512], P(None, 'lon', 'lat')
- flux_sensitivity: float32 [1536, 512], P('lon', 'lat')
The draws below stay inside these ranges and needn't reach their ends.
Inputs may be any that keep to these rules, and one draw needn't show every extreme that they name: `segment_counts`: entry [o, d] is the number of live slots, the first ones, among the 64 slots that retrieval batch o holds for tile d; in every draw one tile gets 64 from every batch, and some batch holds none for some other tile.
All inputs are finite; a program needn't handle non-finite values.
Results may differ from the reference program's by a relative error of at most 0.00013.
Values sent between devices are 32-bit elements; how exact they have to be, the bound alone decides.
A program may use at most 128 MiB of HBM per device.

```python
import math
import jax
import jax.numpy as jnp
from jax import lax

LEV = 72
STEPS = 4
CLON = 48
CLAT = 128
CAP = 64
TILES = 128
NLON = 1536
NLAT = 512
SLOTS = 1048576
N_LON = 32
N_LAT = 4


def draw_segment_counts(key, part):
    key = jax.random.fold_in(key, 7)
    key_one, key_two, key_three, key_four, key_five = jax.random.split(key, 5)
    ceiling = jax.random.randint(key_one, (TILES,), CAP // 4, CAP + 1)
    lowest = ceiling // 2
    raw_bits = jax.random.randint(key_two, (TILES, TILES), 0, 1 << 20)
    counts_drawn = lowest[None, :] + raw_bits % (ceiling - lowest + 1)[None, :]
    busiest = jax.random.randint(key_three, (), 0, TILES)
    counts_drawn = jnp.where(jnp.arange(TILES)[None, :] == busiest, CAP, counts_drawn)
    quiet_tile = (busiest + 1 + jax.random.randint(key_four, (), 0, TILES - 1)) % TILES
    quiet_owner = jax.random.randint(key_five, (), 0, TILES)
    empty_cell = (jnp.arange(TILES)[:, None] == quiet_owner) & (jnp.arange(TILES)[None, :] == quiet_tile)
    counts_drawn = jnp.where(empty_cell, 0, counts_drawn)
    return counts_drawn.astype(jnp.int32)


def plant(drawn, stream_key, low, top_value):
    dims = drawn.shape
    place = [jax.random.randint(jax.random.fold_in(stream_key, axis), (), 0, dims[axis]) for axis in range(len(dims))]
    drawn = drawn.at[tuple(place)].set(low)
    longest = dims.index(max(dims))
    place[longest] = (place[longest] + 1) % dims[longest]
    return drawn.at[tuple(place)].set(top_value)


def level_of(key, dims, shards, low, high):
    loudness = 1.0
    for axis_at, shards_of in shards:
        draws = jax.random.uniform(jax.random.fold_in(jax.random.fold_in(key, 6), axis_at), (shards_of,), jnp.float32, low / len(shards), high / len(shards))
        loudness = loudness * jnp.repeat(jnp.exp(draws), dims[axis_at] // shards_of).reshape((-1,) + (1,) * (len(dims) - 1 - axis_at))
    return loudness


def scatter_about(stream_key, shape, deviation, limit, shards=(), held_as=jnp.bfloat16):
    loudness = level_of(stream_key, shape, shards, -0.22, 0.18) if shards else 1.0
    result = jax.random.normal(stream_key, shape, jnp.float32) * deviation * loudness
    return jnp.minimum(jnp.maximum(result, -limit), limit).astype(held_as)


def setup_inputs(seed: int = 0) -> dict:
    seeds = jax.random.split(jax.random.key(seed), 9)
    return {
        "kernels": jnp.clip(jnp.exp(math.log(2.0) - 2.3025851 * jax.random.uniform(seeds[0], (LEV, SLOTS), jnp.float32) ** level_of(seeds[0], (LEV, SLOTS), ((1, 128),), -0.2, 0.2)), 0.2, 2.0),
        "weighted_residuals": scatter_about(seeds[1], (SLOTS,), 1.0, 6.0, ((0, 128),), jnp.float32),
        "sounding_columns": plant(jax.random.randint(seeds[2], (SLOTS,), 0, CLON * CLAT), jax.random.fold_in(seeds[2], 1), 0, (CLON * CLAT) - 1).astype(jnp.int32),
        "segment_counts": draw_segment_counts(jax.random.fold_in(seeds[8], 71), 0),
        "courant": jnp.clip(jax.random.uniform(seeds[4], (2, LEV, NLON, NLAT), jnp.float32, -0.48, 0.48) * level_of(seeds[4], (2, LEV, NLON, NLAT), ((2, 32), (3, 4)), -0.4, 0.0), -0.48, 0.48),
        "mix_strength": jnp.clip(jnp.exp(math.log(0.6) - 2.4849067 * jax.random.uniform(seeds[5], (NLON, NLAT), jnp.float32) ** level_of(seeds[5], (NLON, NLAT), ((0, 32), (1, 4)), -0.2, 0.2)), 0.05, 0.6),
        "cloud_top": plant(jax.random.randint(seeds[6], (NLON, NLAT), 1, LEV + 1), jax.random.fold_in(seeds[6], 1), 1, LEV).astype(jnp.int32),
        "redistribution": scatter_about(seeds[7], (LEV, LEV), LEV ** -0.5, 0.75, (), jnp.float32),
    }


def reference(kernels, weighted_residuals, sounding_columns, segment_counts, courant, mix_strength, cloud_top, redistribution):
    tile_count = N_LON * N_LAT
    slot_index = jnp.arange(tile_count * tile_count * CAP, dtype=jnp.int32)
    owner_index = slot_index // (tile_count * CAP)
    target_tile = (slot_index // CAP) % tile_count
    is_live = (slot_index % CAP) < segment_counts[owner_index, target_tile]
    forcing = kernels * jnp.where(is_live, weighted_residuals, 0.0)[None, :]
    lon_index = (target_tile // N_LAT) * CLON + sounding_columns // CLAT
    lat_index = (target_tile % N_LAT) * CLAT + sounding_columns % CLAT
    flat_index = (lon_index * NLAT + lat_index).astype(jnp.int32)
    adjoint = jnp.zeros((LEV, NLON * NLAT), jnp.float32).at[:, flat_index].add(forcing)
    adjoint = adjoint.reshape(LEV, NLON, NLAT)
    along_lon = courant[0]
    along_lat = courant[1]
    inside = (jnp.arange(LEV, dtype=jnp.int32)[:, None, None] < cloud_top[None]).astype(jnp.float32)
    flux_sum = jnp.zeros((NLON, NLAT), jnp.float32)
    for step_index in range(STEPS):
        padded = jnp.pad(adjoint, ((0, 0), (0, 0), (1, 1)))
        adjoint = ((1.0 - jnp.abs(along_lon) - jnp.abs(along_lat)) * adjoint
                   + jnp.maximum(along_lon, 0.0) * jnp.roll(adjoint, -1, axis=1)
                   + jnp.maximum(-along_lon, 0.0) * jnp.roll(adjoint, 1, axis=1)
                   + jnp.maximum(along_lat, 0.0) * padded[:, :, 2:]
                   + jnp.maximum(-along_lat, 0.0) * padded[:, :, :-2])
        source = (inside * mix_strength[None] * adjoint).reshape(LEV, -1)
        mixing = jnp.dot(redistribution.T, source, precision=lax.Precision.HIGHEST, preferred_element_type=jnp.float32)
        adjoint = adjoint + inside * mixing.reshape(adjoint.shape)
        flux_sum = flux_sum + adjoint[0]
    return adjoint, flux_sum
```

```python
import itertools

import jax
import jax.numpy as jnp
from jax import lax
from jax.experimental import pallas as pl
from jax.experimental.pallas import tpu as pltpu
from jax.sharding import PartitionSpec as P

STEPS = 4
LEV = 72
CLON = 48
LANES = 128
CHIPS = 64
DEVICES = 128
ROWS = 37
DEPTH = 224

OFFSETS = sorted(
    itertools.product(range(4), repeat=3), key=lambda o: -sum(min(v, 4 - v) for v in o)
)


def coords():
    lon = lax.axis_index("lon")
    lat = lax.axis_index("lat")
    return lon % 4, (lon // 4) % 4, (lat // 2) * 2 + lon // 16, lat % 2


def at_offset(x, y, z, c):
    mx, my, mz, mc = coords()
    x, y, z, c = (mx + x) % 4, (my + y) % 4, (mz + z) % 4, (mc + c) % 2
    return (z % 2) * 16 + y * 4 + x, (z // 2) * 2 + c


def to(lon, lat):
    return {"lon": lon, "lat": lat}


def iota(shape, dim):
    return lax.broadcasted_iota(jnp.int32, shape, dim)


def split(value):
    high = value.astype(jnp.bfloat16).astype(jnp.float32)
    return high, value - high


def kernel(
    kernels,
    residuals,
    columns,
    counts,
    courant,
    strength,
    cloud_top,
    redistribution,
    out,
    flux,
    forcing_in,
    wind,
    send,
    recv,
    state,
    edge,
    from_south,
    from_north,
    halo,
    mixer,
    load_sem,
    wind_sem,
    send_sem,
    recv_sem,
    edge_send,
    edge_recv,
    out_sem,
):
    lon, lat = lax.axis_index("lon"), lax.axis_index("lat")
    core = lat % 2
    load = pltpu.make_async_copy(kernels, forcing_in, load_sem)
    load.start()
    barrier = pltpu.get_barrier_semaphore()

    def greet(k, carry):
        there = at_offset(k % 4, (k // 4) % 4, (k // 16) % 4, k // 64)
        pl.semaphore_signal(barrier, 1, device_id=to(*there))
        return carry

    lax.fori_loop(1, DEVICES, greet, 0)

    def fetch(i, carry):
        for part in range(2):
            pltpu.make_async_copy(
                courant.at[part, :, i, :], wind.at[part, i], wind_sem
            ).start()
        return carry

    lax.fori_loop(0, CLON, fetch, 0)

    lane = iota((8, LANES), 1)
    sub = iota((8, LANES), 0)
    low = lane < 64

    def lo_half(shape):
        return iota(shape, 1) < 64

    load.wait()
    for m, offset in enumerate(OFFSETS):
        there_lon, there_lat = at_offset(*offset, 0)
        chip = there_lon * 2 + there_lat // 2
        one = counts[0, 2 * chip]
        two = counts[0, 2 * chip + 1]
        row = iota((1, LANES), 1)
        live = (row % 64) < jnp.where(row < 64, one, two)
        weight = jnp.where(live, residuals[pl.ds(chip, 1), :], 0.0)
        place = columns[pl.ds(chip, 1), :].astype(jnp.float32)
        start = pl.multiple_of(chip * LANES, LANES)
        value = forcing_in[:, pl.ds(start, LANES)] * weight
        a, b, last = value[0:32], value[32:64], value[64:72]
        half = lo_half((32, LANES))
        turned = pltpu.roll(last, 4, 0)
        tail_0 = jnp.where(low, last, pltpu.roll(turned, 64, 1))
        tail_1 = jnp.where(low, pltpu.roll(last, 64, 1), turned)
        place_8 = jnp.broadcast_to(place, (8, LANES))
        tail_0 = jnp.where(sub == 4, place_8, tail_0)
        tail_1 = jnp.where(sub == 4, pltpu.roll(place_8, 64, 1), tail_1)
        slot_0 = 2 * m + core
        slot_1 = 2 * m + 1 - core
        send[slot_0, 0:32, :] = jnp.where(half, a, pltpu.roll(b, 64, 1))
        send[slot_1, 0:32, :] = jnp.where(half, pltpu.roll(a, 64, 1), b)
        send[slot_0, 32:ROWS, :] = tail_0[0:5]
        send[slot_1, 32:ROWS, :] = tail_1[0:5]
    mine = DEVICES - 2
    recv[mine] = send[mine]

    def block_copy(k, there):
        return pltpu.make_async_remote_copy(
            src_ref=send.at[k],
            dst_ref=recv.at[k],
            send_sem=send_sem.at[k],
            recv_sem=recv_sem.at[k],
            device_id=to(*there),
        )

    pl.semaphore_wait(barrier, DEVICES - 1)
    for m, offset in enumerate(OFFSETS):
        for c in range(2):
            if 2 * m + c != mine:
                block_copy(2 * m + c, at_offset(*offset, c)).start()

    high, rest = split(redistribution[...].T)
    mixer[...] = jnp.concatenate(
        [high, high, rest, jnp.zeros((LEV, DEPTH - 3 * LEV), jnp.float32)], axis=1
    ).astype(jnp.bfloat16)

    def clear(i, carry):
        state[0, i] = jnp.zeros((LEV, LANES), jnp.float32)
        return carry

    lax.fori_loop(1, CLON + 1, clear, 0)

    def paired(k):
        half = lo_half((32, LANES))
        one, two = recv[k, 0:32, :], recv[k + 1, 0:32, :]
        end_1, end_2 = recv[k, 29:ROWS, :], recv[k + 1, 29:ROWS, :]
        top = jnp.where(half, one, pltpu.roll(two, 64, 1))
        bottom = jnp.where(half, pltpu.roll(one, 64, 1), two)
        end_top = jnp.where(low, end_1, pltpu.roll(end_2, 64, 1))
        end_bottom = jnp.where(low, pltpu.roll(end_1, 64, 1), end_2)
        end = jnp.where(sub < 4, pltpu.roll(end_top, 5, 0), pltpu.roll(end_bottom, 1, 0))
        return jnp.concatenate([top, bottom, end], axis=0), end_top[7:8]

    def gather(t, whole):
        first = 4 * t
        for i in range(4):
            if whole or i != mine % 4:
                block_copy(first + i, (lon, lat)).wait_recv()
        one, place_1 = paired(first)
        two, place_2 = paired(first + 2)
        value = jnp.concatenate([one, two], axis=1)
        place = jnp.concatenate([place_1, place_2], axis=1).astype(jnp.int32)
        high, rest = split(value)
        both = jnp.concatenate([high, rest], axis=0).astype(jnp.bfloat16)
        across = place // 256
        within = place % 256
        hot = jnp.where(iota((256, 256), 0) == within, 1.0, 0.0).astype(jnp.bfloat16)
        for q in range(CLON // 2):
            mask = jnp.where(across == q, 1.0, 0.0).astype(jnp.bfloat16)
            put = lax.dot_general(
                both * mask,
                hot,
                (((1,), (1,)), ((), ())),
                preferred_element_type=jnp.float32,
            )
            put = put[:LEV] + put[LEV:]
            state[0, 2 * q + 1] += put[:, :LANES]
            state[0, 2 * q + 2] += put[:, LANES:]

    def gather_step(t, carry):
        gather(t, True)
        return carry

    lax.fori_loop(0, DEVICES // 4 - 1, gather_step, 0)
    gather(DEVICES // 4 - 1, False)

    wide = iota((LEV, LANES), 1)

    def pack(i, value, field):
        return jnp.where(wide // 2 == i, pltpu.roll(value, 2 * i + 1, 1), field)

    edge[0] = jnp.zeros((LEV, LANES), jnp.float32)

    def pack_first(i, carry):
        edge[0] = pack(i, state[0, i + 1], edge[0])
        return carry

    lax.fori_loop(0, CLON, pack_first, 0)
    flux[...] = jnp.zeros((CLON, LANES), jnp.float32)
    pltpu.make_async_copy(wind, wind, wind_sem).wait()

    east, west = (lon + 1) % 32, (lon + 31) % 32
    north, south = (lat + 1) % 4, (lat + 3) % 4

    def edge_copies(s):
        parts = (
            (state.at[s, 1], state.at[s, CLON + 1], (west, lat)),
            (state.at[s, CLON], state.at[s, 0], (east, lat)),
            (edge.at[s], from_south.at[s], (lon, north)),
            (edge.at[s], from_north.at[s], (lon, south)),
        )
        return [
            pltpu.make_async_remote_copy(
                src_ref=source,
                dst_ref=target,
                send_sem=edge_send.at[4 * s + i],
                recv_sem=edge_recv.at[4 * s + i],
                device_id=to(*there),
            )
            for i, (source, target, there) in enumerate(parts)
        ]

    for s in range(STEPS):
        copies = edge_copies(s)
        for copy in copies:
            copy.start()
        for copy in copies:
            copy.wait_recv()
        below = jnp.where(lat > 0, from_south[s], 0.0)
        above = jnp.where(lat < 3, from_north[s], 0.0)
        halo[...] = jnp.where(wide % 2 == 0, below, pltpu.roll(above, LANES - 2, 1))
        if s + 1 < STEPS:
            edge[s + 1] = jnp.zeros((LEV, LANES), jnp.float32)

        def advance(q, carry):
            moved, inside, sources = [], [], []
            for h in range(2):
                i = 2 * q + h
                x = state[s, i + 1]
                a, b = wind[0, i], wind[1, i]
                ends = pltpu.roll(halo[...], (LANES - 2 * i) % LANES, 1)
                after = jnp.where(wide == LANES - 1, ends, pltpu.roll(x, LANES - 1, 1))
                before = jnp.where(wide == 0, ends, pltpu.roll(x, 1, 1))
                along = jnp.where(a > 0, state[s, i + 2], state[s, i])
                over = jnp.where(b > 0, after, before)
                t = x + jnp.abs(a) * (along - x) + jnp.abs(b) * (over - x)
                inner = iota((LEV, LANES), 0) < cloud_top[pl.ds(i, 1), :]
                source = jnp.where(inner, t * strength[pl.ds(i, 1), :], 0.0)
                high, rest = split(source)
                pad = jnp.zeros((DEPTH - 3 * LEV, LANES), jnp.float32)
                moved.append(t)
                inside.append(inner)
                sources.append(jnp.concatenate([high, rest, high, pad], axis=0))
            stack = jnp.concatenate(sources, axis=1).astype(jnp.bfloat16)
            mixed = jnp.dot(mixer[...], stack, preferred_element_type=jnp.float32)
            for h in range(2):
                i = 2 * q + h
                part = mixed[:, h * LANES : (h + 1) * LANES]
                value = moved[h] + jnp.where(inside[h], part, 0.0)
                state[s + 1, i + 1] = value
                flux[pl.ds(i, 1), :] += value[0:1]
                if s + 1 < STEPS:
                    edge[s + 1] = pack(i, value, edge[s + 1])
            return carry

        lax.fori_loop(0, CLON // 2, advance, 0)

    result = pltpu.make_async_copy(state.at[STEPS, pl.ds(1, CLON)], out, out_sem)
    result.start()

    def sent(k, carry):
        block_copy(k, (lon, lat)).wait_send()
        return carry

    lax.fori_loop(0, mine, sent, 0)
    block_copy(DEVICES - 1, (lon, lat)).wait_send()
    for s in range(STEPS):
        for copy in edge_copies(s):
            copy.wait_send()
    result.wait()


def on_device(
    kernels,
    weighted_residuals,
    sounding_columns,
    segment_counts,
    courant,
    mix_strength,
    cloud_top,
    redistribution,
):
    in_vmem = pl.BlockSpec(memory_space=pltpu.VMEM)
    anywhere = pl.BlockSpec(memory_space=pl.ANY)
    f32 = jnp.float32
    field, flux = pl.pallas_call(
        kernel,
        out_shape=(
            jax.ShapeDtypeStruct((CLON, LEV, LANES), f32),
            jax.ShapeDtypeStruct((CLON, LANES), f32),
        ),
        in_specs=[
            anywhere,
            in_vmem,
            in_vmem,
            pl.BlockSpec(memory_space=pltpu.SMEM),
            anywhere,
            in_vmem,
            in_vmem,
            in_vmem,
        ],
        out_specs=(anywhere, in_vmem),
        scratch_shapes=[
            pltpu.VMEM((LEV, CHIPS * LANES), f32),
            pltpu.VMEM((2, CLON, LEV, LANES), f32),
            pltpu.VMEM((DEVICES, ROWS, LANES), f32),
            pltpu.VMEM((DEVICES, ROWS, LANES), f32),
            pltpu.VMEM((STEPS + 1, CLON + 2, LEV, LANES), f32),
            pltpu.VMEM((STEPS, LEV, LANES), f32),
            pltpu.VMEM((STEPS, LEV, LANES), f32),
            pltpu.VMEM((STEPS, LEV, LANES), f32),
            pltpu.VMEM((LEV, LANES), f32),
            pltpu.VMEM((LEV, DEPTH), jnp.bfloat16),
            pltpu.SemaphoreType.DMA,
            pltpu.SemaphoreType.DMA,
            pltpu.SemaphoreType.DMA((DEVICES,)),
            pltpu.SemaphoreType.DMA((DEVICES,)),
            pltpu.SemaphoreType.DMA((4 * STEPS,)),
            pltpu.SemaphoreType.DMA((4 * STEPS,)),
            pltpu.SemaphoreType.DMA,
        ],
        compiler_params=pltpu.CompilerParams(
            collective_id=0, has_side_effects=True, vmem_limit_bytes=50 * 2**20
        ),
    )(
        kernels,
        weighted_residuals.reshape(CHIPS, LANES),
        sounding_columns.reshape(CHIPS, LANES),
        segment_counts,
        courant,
        mix_strength,
        cloud_top,
        redistribution,
    )
    return field.transpose(1, 0, 2), flux


def solution(mesh):
    return jax.shard_map(
        on_device,
        mesh=mesh,
        in_specs=(
            P(None, ("lon", "lat")),
            P(("lon", "lat")),
            P(("lon", "lat")),
            P(("lon", "lat"), None),
            P(None, None, "lon", "lat"),
            P("lon", "lat"),
            P("lon", "lat"),
            P(),
        ),
        out_specs=(P(None, "lon", "lat"), P("lon", "lat")),
        check_vma=False,
    )
```

```python
import itertools

import jax
import jax.numpy as jnp
from jax import lax
from jax.experimental import pallas as pl
from jax.experimental.pallas import tpu as pltpu
from jax.sharding import PartitionSpec as P

STEPS = 4
LEV = 72
CLON = 48
LANES = 128
CHIPS = 64
DEVICES = 128
ROWS = 37
BLOCKS = 8
UNROLL = 6
DEPTH = 224

OFFSETS = sorted(
    itertools.product(range(4), repeat=3), key=lambda o: -sum(min(v, 4 - v) for v in o)
)


def coords():
    lon = lax.axis_index("lon")
    lat = lax.axis_index("lat")
    return lon % 4, (lon // 4) % 4, (lat // 2) * 2 + lon // 16, lat % 2


def placer():
    x, y, z, c = coords()
    xs = [lax.rem(x + d, 4) for d in range(4)]
    ys = [lax.rem(y + d, 4) * 4 for d in range(4)]
    zs = [lax.rem(z + d, 4) for d in range(4)]
    inner = [lax.rem(v, 2) * 16 for v in zs]
    outer = [lax.div(v, 2) * 2 for v in zs]
    cores = [c, 1 - c]

    def place(dx, dy, dz, dc):
        return inner[dz] + ys[dy] + xs[dx], outer[dz] + cores[dc]

    return place


def to(lon, lat):
    return {"lon": lon, "lat": lat}


def iota(shape, dim):
    return lax.broadcasted_iota(jnp.int32, shape, dim)


def split(value):
    high = value.astype(jnp.bfloat16).astype(jnp.float32)
    return high, value - high


def kernel(
    kernels,
    residuals_in,
    columns_in,
    counts_in,
    courant,
    strength_in,
    cloud_top_in,
    redistribution_in,
    out,
    flux,
    residuals,
    columns,
    counts,
    strength,
    cloud_top,
    redistribution,
    small_sem,
    forcing_in,
    wind,
    send,
    recv,
    state_0,
    state_1,
    state_2,
    state_3,
    state_4,
    edge,
    from_south,
    from_north,
    halo,
    mixer,
    load_sem,
    wind_sem,
    send_sem,
    recv_sem,
    edge_send,
    edge_recv,
    out_sem,
):
    states = (state_0, state_1, state_2, state_3, state_4)
    lon, lat = lax.axis_index("lon"), lax.axis_index("lat")
    core = lat % 2
    at_offset = placer()
    load = pltpu.make_async_copy(kernels, forcing_in, load_sem)
    load.start()
    small = [
        pltpu.make_async_copy(source, target, small_sem.at[i])
        for i, (source, target) in enumerate(
            (
                (counts_in, counts),
                (residuals_in, residuals),
                (columns_in, columns),
                (strength_in, strength),
                (cloud_top_in, cloud_top),
                (redistribution_in, redistribution),
            )
        )
    ]
    for copy in small:
        copy.start()
    barrier = pltpu.get_barrier_semaphore()
    for offset in OFFSETS:
        for c in range(2):
            if any(offset) or c:
                pl.semaphore_signal(barrier, 1, device_id=to(*at_offset(*offset, c)))

    def fetch(i, carry):
        for part in range(2):
            pltpu.make_async_copy(
                courant.at[part, :, i, :], wind.at[part, i], wind_sem
            ).start()
        return carry

    lax.fori_loop(0, CLON, fetch, 0)

    lane = iota((8, LANES), 1)
    sub = iota((8, LANES), 0)
    low = lane < 64

    def lo_half(shape):
        return iota(shape, 1) < 64

    for copy in small:
        copy.wait()
    load.wait()
    for m, offset in enumerate(OFFSETS):
        there_lon, there_lat = at_offset(*offset, 0)
        chip = there_lon * 2 + there_lat // 2
        one = counts[0, 2 * chip]
        two = counts[0, 2 * chip + 1]
        row = iota((1, LANES), 1)
        live = (row % 64) < jnp.where(row < 64, one, two)
        weight = jnp.where(live, residuals[pl.ds(chip, 1), :], 0.0)
        place = columns[pl.ds(chip, 1), :].astype(jnp.float32)
        start = pl.multiple_of(chip * LANES, LANES)
        value = forcing_in[:, pl.ds(start, LANES)] * weight
        a, b, last = value[0:32], value[32:64], value[64:72]
        half = lo_half((32, LANES))
        turned = pltpu.roll(last, 4, 0)
        tail_0 = jnp.where(low, last, pltpu.roll(turned, 64, 1))
        tail_1 = jnp.where(low, pltpu.roll(last, 64, 1), turned)
        place_8 = jnp.broadcast_to(place, (8, LANES))
        tail_0 = jnp.where(sub == 4, place_8, tail_0)
        tail_1 = jnp.where(sub == 4, pltpu.roll(place_8, 64, 1), tail_1)
        slot_0 = 2 * m + core
        slot_1 = 2 * m + 1 - core
        send[slot_0, 0:32, :] = jnp.where(half, a, pltpu.roll(b, 64, 1))
        send[slot_1, 0:32, :] = jnp.where(half, pltpu.roll(a, 64, 1), b)
        send[slot_0, 32:ROWS, :] = tail_0[0:5]
        send[slot_1, 32:ROWS, :] = tail_1[0:5]
    mine = DEVICES - 2
    recv[mine] = send[mine]

    def block_copy(k, there):
        return pltpu.make_async_remote_copy(
            src_ref=send.at[k],
            dst_ref=recv.at[k],
            send_sem=send_sem.at[k],
            recv_sem=recv_sem.at[k],
            device_id=to(*there),
        )

    pl.semaphore_wait(barrier, DEVICES - 1)
    for m, offset in enumerate(OFFSETS):
        for c in range(2):
            if 2 * m + c != mine:
                block_copy(2 * m + c, at_offset(*offset, c)).start()

    high, rest = split(redistribution[...].T)
    mixer[...] = jnp.concatenate(
        [high, high, rest, jnp.zeros((LEV, DEPTH - 3 * LEV), jnp.float32)], axis=1
    ).astype(jnp.bfloat16)

    def clear(i, carry):
        state_0[i] = jnp.zeros((LEV, LANES), jnp.float32)
        return carry

    lax.fori_loop(1, CLON + 1, clear, 0)

    def paired(k):
        half = lo_half((32, LANES))
        one, two = recv[k, 0:32, :], recv[k + 1, 0:32, :]
        end_1, end_2 = recv[k, 29:ROWS, :], recv[k + 1, 29:ROWS, :]
        top = jnp.where(half, one, pltpu.roll(two, 64, 1))
        bottom = jnp.where(half, pltpu.roll(one, 64, 1), two)
        end_top = jnp.where(low, end_1, pltpu.roll(end_2, 64, 1))
        end_bottom = jnp.where(low, pltpu.roll(end_1, 64, 1), end_2)
        end = jnp.where(sub < 4, pltpu.roll(end_top, 5, 0), pltpu.roll(end_bottom, 1, 0))
        return jnp.concatenate([top, bottom, end], axis=0), end_top[7:8]

    def gather(t, whole):
        first = BLOCKS * t
        values, places = [], []
        for i in range(BLOCKS):
            if whole or i != mine % BLOCKS:
                block_copy(first + i, (lon, lat)).wait_recv()
        for i in range(0, BLOCKS, 2):
            value, place = paired(first + i)
            high, rest = split(value)
            values.append(jnp.concatenate([high, rest], axis=0))
            places.append(place)
        both = jnp.concatenate(values, axis=1).astype(jnp.bfloat16)
        place = jnp.concatenate(places, axis=1).astype(jnp.int32)
        across = lax.div(place, 256)
        within = lax.rem(place, 256)
        hot = iota((256, BLOCKS * 64), 0) == within
        hot = jnp.where(hot, 1.0, 0.0).astype(jnp.bfloat16)
        for q in range(0, CLON // 2, 2):
            masks = [
                jnp.where(across == q + h, 1.0, 0.0).astype(jnp.bfloat16) for h in range(2)
            ]
            put = lax.dot_general(
                jnp.concatenate([both * mask for mask in masks], axis=0),
                hot,
                (((1,), (1,)), ((), ())),
                preferred_element_type=jnp.float32,
            )
            for h in range(2):
                part = put[2 * h * LEV : (2 * h + 1) * LEV]
                part = part + put[(2 * h + 1) * LEV : (2 * h + 2) * LEV]
                state_0[2 * (q + h) + 1] += part[:, :LANES]
                state_0[2 * (q + h) + 2] += part[:, LANES:]

    def gather_step(t, carry):
        gather(t, True)
        return carry

    lax.fori_loop(0, DEVICES // BLOCKS - 1, gather_step, 0)
    gather(DEVICES // BLOCKS - 1, False)

    wide = iota((LEV, LANES), 1)

    def pack(i, value, field):
        return jnp.where(wide // 2 == i, pltpu.roll(value, 2 * i + 1, 1), field)

    def pack_first(g, field):
        for k in range(UNROLL):
            i = g * UNROLL + k
            field = pack(i, state_0[i + 1], field)
        return field

    nothing = jnp.zeros((LEV, LANES), jnp.float32)
    edge[0] = lax.fori_loop(0, CLON // UNROLL, pack_first, nothing)
    flux[...] = jnp.zeros((CLON, LANES), jnp.float32)
    pltpu.make_async_copy(wind, wind, wind_sem).wait()

    east, west = (lon + 1) % 32, (lon + 31) % 32
    north, south = (lat + 1) % 4, (lat + 3) % 4

    def edge_copies(s):
        parts = (
            (states[s].at[1], states[s].at[CLON + 1], (west, lat)),
            (states[s].at[CLON], states[s].at[0], (east, lat)),
            (edge.at[s], from_south.at[s], (lon, north)),
            (edge.at[s], from_north.at[s], (lon, south)),
        )
        return [
            pltpu.make_async_remote_copy(
                src_ref=source,
                dst_ref=target,
                send_sem=edge_send.at[4 * s + i],
                recv_sem=edge_recv.at[4 * s + i],
                device_id=to(*there),
            )
            for i, (source, target, there) in enumerate(parts)
        ]

    for s in range(STEPS):
        copies = edge_copies(s)
        for copy in copies:
            copy.start()
        for copy in copies:
            copy.wait_recv()
        below = jnp.where(lat > 0, from_south[s], 0.0)
        above = jnp.where(lat < 3, from_north[s], 0.0)
        halo[...] = jnp.where(wide % 2 == 0, below, pltpu.roll(above, LANES - 2, 1))
        now, later = states[s], states[s + 1]

        def advance(g, field):
            for k in range(UNROLL):
                moved, inside, sources = [], [], []
                for h in range(2):
                    i = 2 * (g * UNROLL + k) + h
                    x = now[i + 1]
                    a, b = wind[0, i], wind[1, i]
                    ends = pltpu.roll(halo[...], lax.rem(LANES - 2 * i, LANES), 1)
                    after = pltpu.roll(x, LANES - 1, 1)
                    after = jnp.where(wide == LANES - 1, ends, after)
                    before = jnp.where(wide == 0, ends, pltpu.roll(x, 1, 1))
                    along = jnp.where(a > 0, now[i + 2], now[i])
                    over = jnp.where(b > 0, after, before)
                    t = x + jnp.abs(a) * (along - x) + jnp.abs(b) * (over - x)
                    inner = iota((LEV, LANES), 0) < cloud_top[pl.ds(i, 1), :]
                    source = jnp.where(inner, t * strength[pl.ds(i, 1), :], 0.0)
                    high, rest = split(source)
                    pad = jnp.zeros((DEPTH - 3 * LEV, LANES), jnp.float32)
                    moved.append(t)
                    inside.append(inner)
                    sources.append(jnp.concatenate([high, rest, high, pad], axis=0))
                stack = jnp.concatenate(sources, axis=1).astype(jnp.bfloat16)
                mixed = jnp.dot(mixer[...], stack, preferred_element_type=jnp.float32)
                for h in range(2):
                    i = 2 * (g * UNROLL + k) + h
                    part = mixed[:, h * LANES : (h + 1) * LANES]
                    value = moved[h] + jnp.where(inside[h], part, 0.0)
                    later[i + 1] = value
                    flux[pl.ds(i, 1), :] += value[0:1]
                    if s + 1 < STEPS:
                        field = pack(i, value, field)
            return field

        packed = lax.fori_loop(0, CLON // 2 // UNROLL, advance, nothing)
        if s + 1 < STEPS:
            edge[s + 1] = packed

    result = pltpu.make_async_copy(state_4.at[pl.ds(1, CLON)], out, out_sem)
    result.start()

    def sent(k, carry):
        block_copy(k, (lon, lat)).wait_send()
        return carry

    lax.fori_loop(0, mine, sent, 0)
    block_copy(DEVICES - 1, (lon, lat)).wait_send()
    for s in range(STEPS):
        for copy in edge_copies(s):
            copy.wait_send()
    result.wait()


def on_device(
    kernels,
    weighted_residuals,
    sounding_columns,
    segment_counts,
    courant,
    mix_strength,
    cloud_top,
    redistribution,
):
    in_vmem = pl.BlockSpec(memory_space=pltpu.VMEM)
    anywhere = pl.BlockSpec(memory_space=pl.ANY)
    f32 = jnp.float32
    field, flux = pl.pallas_call(
        kernel,
        out_shape=(
            jax.ShapeDtypeStruct((CLON, LEV, LANES), f32),
            jax.ShapeDtypeStruct((CLON, LANES), f32),
        ),
        in_specs=[pl.BlockSpec(memory_space=pltpu.HBM)] * 8,
        out_specs=(anywhere, in_vmem),
        scratch_shapes=[
            pltpu.VMEM((CHIPS, LANES), f32),
            pltpu.VMEM((CHIPS, LANES), jnp.int32),
            pltpu.SMEM((1, DEVICES), jnp.int32),
            pltpu.VMEM((CLON, LANES), f32),
            pltpu.VMEM((CLON, LANES), jnp.int32),
            pltpu.VMEM((LEV, LEV), f32),
            pltpu.SemaphoreType.DMA((6,)),
            pltpu.VMEM((LEV, CHIPS * LANES), f32),
            pltpu.VMEM((2, CLON, LEV, LANES), f32),
            pltpu.VMEM((DEVICES, ROWS, LANES), f32),
            pltpu.VMEM((DEVICES, ROWS, LANES), f32),
            *[pltpu.VMEM((CLON + 2, LEV, LANES), f32) for _ in range(STEPS + 1)],
            pltpu.VMEM((STEPS, LEV, LANES), f32),
            pltpu.VMEM((STEPS, LEV, LANES), f32),
            pltpu.VMEM((STEPS, LEV, LANES), f32),
            pltpu.VMEM((LEV, LANES), f32),
            pltpu.VMEM((LEV, DEPTH), jnp.bfloat16),
            pltpu.SemaphoreType.DMA,
            pltpu.SemaphoreType.DMA,
            pltpu.SemaphoreType.DMA((DEVICES,)),
            pltpu.SemaphoreType.DMA((DEVICES,)),
            pltpu.SemaphoreType.DMA((4 * STEPS,)),
            pltpu.SemaphoreType.DMA((4 * STEPS,)),
            pltpu.SemaphoreType.DMA,
        ],
        compiler_params=pltpu.CompilerParams(
            collective_id=0, has_side_effects=True, vmem_limit_bytes=60 * 2**20
        ),
    )(
        kernels,
        weighted_residuals.reshape(CHIPS, LANES),
        sounding_columns.reshape(CHIPS, LANES),
        segment_counts,
        courant,
        mix_strength,
        cloud_top,
        redistribution,
    )
    return field.transpose(1, 0, 2), flux


def solution(mesh):
    return jax.shard_map(
        on_device,
        mesh=mesh,
        in_specs=(
            P(None, ("lon", "lat")),
            P(("lon", "lat")),
            P(("lon", "lat")),
            P(("lon", "lat"), None),
            P(None, None, "lon", "lat"),
            P("lon", "lat"),
            P("lon", "lat"),
            P(),
        ),
        out_specs=(P(None, "lon", "lat"), P("lon", "lat")),
        check_vma=False,
    )
```

```python
import itertools

import jax
import jax.numpy as jnp
from jax import lax
from jax.experimental import pallas as pl
from jax.experimental.pallas import tpu as pltpu
from jax.sharding import PartitionSpec as P

STEPS = 4
LEV = 72
CLON = 48
LANES = 128
CHIPS = 64
DEVICES = 128
ROWS = 37
BLOCKS = 8
UNROLL = 6
PAIRS = 11
FIRST = 64
GROUP = 16
DEPTH = 224

OFFSETS = sorted(
    itertools.product(range(4), repeat=3), key=lambda o: sum(min(v, 4 - v) for v in o)
)
OFFSETS = OFFSETS[1:] + OFFSETS[:1]


def coords():
    lon = lax.axis_index("lon")
    lat = lax.axis_index("lat")
    return lon % 4, (lon // 4) % 4, (lat // 2) * 2 + lon // 16, lat % 2


def placer():
    x, y, z, c = coords()
    xs = [lax.rem(x + d, 4) for d in range(4)]
    ys = [lax.rem(y + d, 4) * 4 for d in range(4)]
    zs = [lax.rem(z + d, 4) for d in range(4)]
    inner = [lax.rem(v, 2) * 16 for v in zs]
    outer = [lax.div(v, 2) * 2 for v in zs]
    cores = [c, 1 - c]

    def place(dx, dy, dz, dc):
        return inner[dz] + ys[dy] + xs[dx], outer[dz] + cores[dc]

    return place


def to(lon, lat):
    return {"lon": lon, "lat": lat}


def iota(shape, dim):
    return lax.broadcasted_iota(jnp.int32, shape, dim)


def split(value):
    high = value.astype(jnp.bfloat16).astype(jnp.float32)
    return high, value - high


def lanes(low, high):
    lane = iota((1, LANES), 1)
    return (lane == low) | (lane == high)


def pack_ends(i, value, field):
    return jnp.where(lanes(2 * i, 2 * i + 1), pltpu.roll(value, 2 * i + 1, 1), field)


def pack_near(i, value, field):
    return jnp.where(lanes(2 * i, 2 * i + 3), pltpu.roll(value, 2 * i + 2, 1), field)


def put_ends(i, field, value):
    ends = pltpu.roll(field, LANES - 1 - 2 * i, 1)
    return jnp.where(lanes(LANES - 1, 0), ends, value)


def transport(x, east, west, north, south, a, b):
    along = jnp.where(a > 0, east, west)
    over = jnp.where(b > 0, north, south)
    return x + jnp.abs(a) * (along - x) + jnp.abs(b) * (over - x)


def convect(columns, mixer):
    sources, inside = [], []
    for field, top, strength in columns:
        inner = iota((LEV, LANES), 0) < top
        high, rest = split(jnp.where(inner, field * strength, 0.0))
        pad = jnp.zeros((DEPTH - 3 * LEV, LANES), jnp.float32)
        sources.append(jnp.concatenate([high, rest, high, pad], axis=0))
        inside.append(inner)
    stack = jnp.concatenate(sources, axis=1).astype(jnp.bfloat16)
    mixed = jnp.dot(mixer, stack, preferred_element_type=jnp.float32)
    return [
        column[0] + jnp.where(inner, mixed[:, h * LANES : (h + 1) * LANES], 0.0)
        for h, (column, inner) in enumerate(zip(columns, inside))
    ]


def kernel(
    kernels,
    residuals_in,
    columns_in,
    counts_in,
    courant,
    strength_in,
    cloud_top_in,
    redistribution_in,
    out,
    flux,
    residuals,
    columns,
    counts,
    strength,
    cloud_top,
    redistribution,
    small_sem,
    forcing_in,
    wind,
    send,
    recv,
    state_0,
    state_1,
    state_2,
    state_3,
    state_4,
    edge,
    from_south,
    from_north,
    strip_wind,
    strip_strength,
    strip_top,
    mixer,
    load_sem,
    wind_sem,
    send_sem,
    recv_sem,
    edge_send,
    edge_recv,
):
    states = (state_0, state_1, state_2, state_3, state_4)
    lon, lat = lax.axis_index("lon"), lax.axis_index("lat")
    core = lat % 2
    at_offset = placer()
    chips = [at_offset(*offset, 0) for offset in OFFSETS]
    chips = [there_lon * 2 + lax.div(there_lat, 2) for there_lon, there_lat in chips]

    def load(m):
        at = pl.ds(pl.multiple_of(chips[m] * LANES, LANES), LANES)
        return pltpu.make_async_copy(
            kernels.at[:, at], forcing_in.at[:, at], load_sem.at[m]
        )

    small = [
        pltpu.make_async_copy(source, target, small_sem.at[i])
        for i, (source, target) in enumerate(
            (
                (counts_in, counts),
                (residuals_in, residuals),
                (columns_in, columns),
                (strength_in, strength),
                (cloud_top_in, cloud_top),
                (redistribution_in, redistribution),
            )
        )
    ]
    for copy in small:
        copy.start()
    for m in range(CHIPS):
        load(m).start()
    barrier = pltpu.get_barrier_semaphore()
    for offset in OFFSETS:
        for c in range(2):
            if any(offset) or c:
                pl.semaphore_signal(barrier, 1, device_id=to(*at_offset(*offset, c)))

    def fetch(i, carry):
        for part in range(2):
            pltpu.make_async_copy(
                courant.at[part, :, i, :], wind.at[part, i], wind_sem
            ).start()
        return carry

    lax.fori_loop(0, CLON, fetch, 0)

    lane = iota((8, LANES), 1)
    sub = iota((8, LANES), 0)
    low = lane < 64

    def lo_half(shape):
        return iota(shape, 1) < 64

    def block_copy(k, there):
        return pltpu.make_async_remote_copy(
            src_ref=send.at[k],
            dst_ref=recv.at[k],
            send_sem=send_sem.at[k],
            recv_sem=recv_sem.at[k],
            device_id=to(*there),
        )

    mine = DEVICES - 2

    def send_to(m):
        load(m).wait()
        chip = chips[m]
        one = counts[0, 2 * chip]
        two = counts[0, 2 * chip + 1]
        row = iota((1, LANES), 1)
        live = (row % 64) < jnp.where(row < 64, one, two)
        weight = jnp.where(live, residuals[pl.ds(chip, 1), :], 0.0)
        place = columns[pl.ds(chip, 1), :].astype(jnp.float32)
        start = pl.multiple_of(chip * LANES, LANES)
        value = forcing_in[:, pl.ds(start, LANES)] * weight
        a, b, last = value[0:32], value[32:64], value[64:72]
        half = lo_half((32, LANES))
        turned = pltpu.roll(last, 4, 0)
        tail_0 = jnp.where(low, last, pltpu.roll(turned, 64, 1))
        tail_1 = jnp.where(low, pltpu.roll(last, 64, 1), turned)
        place_8 = jnp.broadcast_to(place, (8, LANES))
        tail_0 = jnp.where(sub == 4, place_8, tail_0)
        tail_1 = jnp.where(sub == 4, pltpu.roll(place_8, 64, 1), tail_1)
        slot_0 = 2 * m + core
        slot_1 = 2 * m + 1 - core
        send[slot_0, 0:32, :] = jnp.where(half, a, pltpu.roll(b, 64, 1))
        send[slot_1, 0:32, :] = jnp.where(half, pltpu.roll(a, 64, 1), b)
        send[slot_0, 32:ROWS, :] = tail_0[0:5]
        send[slot_1, 32:ROWS, :] = tail_1[0:5]
        for c in range(2):
            if 2 * m + c != mine:
                block_copy(2 * m + c, at_offset(*OFFSETS[m], c)).start()
            else:
                recv[mine] = send[mine]

    for copy in small:
        copy.wait()
    pl.semaphore_wait(barrier, DEVICES - 1)
    for m in range(FIRST):
        send_to(m)

    high, rest = split(redistribution[...].T)
    mixer[...] = jnp.concatenate(
        [high, high, rest, jnp.zeros((LEV, DEPTH - 3 * LEV), jnp.float32)], axis=1
    ).astype(jnp.bfloat16)

    def clear(i, carry):
        state_0[i] = jnp.zeros((LEV, LANES), jnp.float32)
        return carry

    lax.fori_loop(1, CLON + 1, clear, 0)

    pltpu.make_async_copy(wind, wind, wind_sem).wait()
    nothing = jnp.zeros((LEV, LANES), jnp.float32)
    few = jnp.zeros((8, LANES), jnp.float32)

    def pack_static(g, fields):
        a, b, c, d = fields
        for k in range(UNROLL):
            i = g * UNROLL + k
            a = pack_ends(i, wind[0, i], a)
            b = pack_ends(i, wind[1, i], b)
            row = strength[pl.ds(i, 1), :]
            c = pack_ends(i, jnp.broadcast_to(row, (8, LANES)), c)
            row = cloud_top[pl.ds(i, 1), :].astype(jnp.float32)
            d = pack_ends(i, jnp.broadcast_to(row, (8, LANES)), d)
        return a, b, c, d

    strips = lax.fori_loop(0, CLON // UNROLL, pack_static, (nothing, nothing, few, few))
    strip_wind[0], strip_wind[1], strip_strength[...] = strips[:3]
    strip_top[...] = strips[3].astype(jnp.int32)

    def paired(k):
        half = lo_half((32, LANES))
        one, two = recv[k, 0:32, :], recv[k + 1, 0:32, :]
        end_1, end_2 = recv[k, 29:ROWS, :], recv[k + 1, 29:ROWS, :]
        top = jnp.where(half, one, pltpu.roll(two, 64, 1))
        bottom = jnp.where(half, pltpu.roll(one, 64, 1), two)
        end_top = jnp.where(low, end_1, pltpu.roll(end_2, 64, 1))
        end_bottom = jnp.where(low, pltpu.roll(end_1, 64, 1), end_2)
        end = jnp.where(sub < 4, pltpu.roll(end_top, 5, 0), pltpu.roll(end_bottom, 1, 0))
        return jnp.concatenate([top, bottom, end], axis=0), end_top[7:8]

    def gather(t, whole):
        first = BLOCKS * t
        values, places = [], []
        for i in range(BLOCKS):
            if whole or i != mine % BLOCKS:
                block_copy(first + i, (lon, lat)).wait_recv()
        for i in range(0, BLOCKS, 2):
            value, place = paired(first + i)
            high, rest = split(value)
            values.append(jnp.concatenate([high, rest], axis=0))
            places.append(place)
        both = jnp.concatenate(values, axis=1).astype(jnp.bfloat16)
        place = jnp.concatenate(places, axis=1).astype(jnp.int32)
        across = lax.div(place, 256)
        within = lax.rem(place, 256)
        hot = iota((256, BLOCKS * 64), 0) == within
        hot = jnp.where(hot, 1.0, 0.0).astype(jnp.bfloat16)
        for q in range(0, CLON // 2, 2):
            masks = [
                jnp.where(across == q + h, 1.0, 0.0).astype(jnp.bfloat16) for h in range(2)
            ]
            put = lax.dot_general(
                jnp.concatenate([both * mask for mask in masks], axis=0),
                hot,
                (((1,), (1,)), ((), ())),
                preferred_element_type=jnp.float32,
            )
            for h in range(2):
                part = put[2 * h * LEV : (2 * h + 1) * LEV]
                part = part + put[(2 * h + 1) * LEV : (2 * h + 2) * LEV]
                state_0[2 * (q + h) + 1] += part[:, :LANES]
                state_0[2 * (q + h) + 2] += part[:, LANES:]

    def gather_step(t, carry):
        gather(t, True)
        return carry

    ahead = FIRST
    for t in range(0, DEVICES // BLOCKS, GROUP):
        whole = t + GROUP < DEVICES // BLOCKS
        lax.fori_loop(t, t + GROUP - (0 if whole else 1), gather_step, 0)
        for m in range(ahead, min(ahead + GROUP * BLOCKS // 2, CHIPS)):
            send_to(m)
        ahead += GROUP * BLOCKS // 2
    gather(DEVICES // BLOCKS - 1, False)

    def pack_first(g, fields):
        ends, near = fields
        for k in range(UNROLL):
            i = g * UNROLL + k
            value = state_0[i + 1]
            ends, near = pack_ends(i, value, ends), pack_near(i, value, near)
        return ends, near

    first = lax.fori_loop(0, CLON // UNROLL, pack_first, (nothing, nothing))
    edge[0], near = first
    flux[...] = jnp.zeros((CLON, LANES), jnp.float32)
    flux_ends = few

    east, west = lax.rem(lon + 1, 32), lax.rem(lon + 31, 32)
    north, south = lax.rem(lat + 1, 4), lax.rem(lat + 3, 4)

    def edge_copies(s):
        parts = (
            (edge.at[s], from_south.at[s], (lon, north)),
            (edge.at[s], from_north.at[s], (lon, south)),
            (states[s].at[1], states[s].at[CLON + 1], (west, lat)),
            (states[s].at[CLON], states[s].at[0], (east, lat)),
        )
        return [
            pltpu.make_async_remote_copy(
                src_ref=source,
                dst_ref=target,
                send_sem=edge_send.at[4 * s + i],
                recv_sem=edge_recv.at[4 * s + i],
                device_id=to(*there),
            )
            for i, (source, target, there) in enumerate(parts)
        ]

    even = lax.rem(iota((1, LANES), 1), 2) == 0

    for s in range(STEPS):
        now, later = states[s], states[s + 1]
        for copy in edge_copies(s):
            copy.start()

        def row(i, ends):
            x = now[i + 1] if ends is None else put_ends(i, ends, now[i + 1])
            after, before = pltpu.roll(x, LANES - 1, 1), pltpu.roll(x, 1, 1)
            moved = transport(
                x, now[i + 2], now[i], after, before, wind[0, i], wind[1, i]
            )
            return moved, cloud_top[pl.ds(i, 1), :], strength[pl.ds(i, 1), :]

        def advance_pair(i, field):
            ends = edge[s] if s else None
            values = convect([row(i, ends), row(i + 1, ends)], mixer[...])
            for h, value in enumerate(values):
                later[i + h + 1] = value
                flux[pl.ds(i + h, 1), :] += value[0:1]
                field = pack_near(i + h, value, field)
            return field

        def advance(g, field):
            for k in range(PAIRS):
                field = advance_pair(1 + 2 * (g * PAIRS + k), field)
            return field

        groups = (CLON - 2) // 2 // PAIRS
        next_near = lax.fori_loop(0, groups, advance, nothing)
        for i in range(1 + 2 * groups * PAIRS, CLON - 1, 2):
            next_near = advance_pair(i, next_near)

        for copy in edge_copies(s):
            copy.wait_recv()
        x = edge[s]
        near = jnp.where(even, near, pltpu.roll(near, LANES - 2, 1))
        above = jnp.where(lat < 3, from_north[s], 0.0)
        below = jnp.where(lat > 0, from_south[s], 0.0)
        after = jnp.where(even, pltpu.roll(above, LANES - 1, 1), near)
        before = jnp.where(even, near, pltpu.roll(below, 1, 1))
        around = pack_ends(CLON, now[CLON + 1], pack_ends(63, now[0], x))
        moved = transport(
            x,
            pltpu.roll(around, LANES - 2, 1),
            pltpu.roll(around, 2, 1),
            after,
            before,
            strip_wind[0],
            strip_wind[1],
        )
        strip = (moved, strip_top[0:1, :], strip_strength[0:1, :])
        ends, one, two = convect([strip, row(0, None), row(CLON - 1, None)], mixer[...])
        edge[s + 1] = ends
        flux_ends = flux_ends + ends[0:8]
        for i, value in ((0, one), (CLON - 1, two)):
            later[i + 1] = put_ends(i, ends, value)
            flux[pl.ds(i, 1), :] += value[0:1]
            next_near = pack_near(i, value, next_near)
        near = next_near

    def finish(g, carry):
        for k in range(UNROLL):
            i = g * UNROLL + k
            out[i] = put_ends(i, edge[STEPS], state_4[i + 1])
            total = jnp.broadcast_to(flux[pl.ds(i, 1), :], (8, LANES))
            flux[pl.ds(i, 1), :] = put_ends(i, flux_ends, total)[0:1]
        return carry

    lax.fori_loop(0, CLON // UNROLL, finish, 0)

    def sent(k, carry):
        block_copy(k, (lon, lat)).wait_send()
        return carry

    lax.fori_loop(0, mine, sent, 0)
    block_copy(DEVICES - 1, (lon, lat)).wait_send()
    for s in range(STEPS):
        for copy in edge_copies(s):
            copy.wait_send()


def on_device(
    kernels,
    weighted_residuals,
    sounding_columns,
    segment_counts,
    courant,
    mix_strength,
    cloud_top,
    redistribution,
):
    in_vmem = pl.BlockSpec(memory_space=pltpu.VMEM)
    f32 = jnp.float32
    field, flux = pl.pallas_call(
        kernel,
        out_shape=(
            pltpu.VMEM((CLON, LEV, LANES), f32),
            pltpu.VMEM((CLON, LANES), f32),
        ),
        in_specs=[pl.BlockSpec(memory_space=pl.ANY)] * 8,
        out_specs=(in_vmem, in_vmem),
        scratch_shapes=[
            pltpu.VMEM((CHIPS, LANES), f32),
            pltpu.VMEM((CHIPS, LANES), jnp.int32),
            pltpu.SMEM((1, DEVICES), jnp.int32),
            pltpu.VMEM((CLON, LANES), f32),
            pltpu.VMEM((CLON, LANES), jnp.int32),
            pltpu.VMEM((LEV, LEV), f32),
            pltpu.SemaphoreType.DMA((6,)),
            pltpu.VMEM((LEV, CHIPS * LANES), f32),
            pltpu.VMEM((2, CLON, LEV, LANES), f32),
            pltpu.VMEM((DEVICES, ROWS, LANES), f32),
            pltpu.VMEM((DEVICES, ROWS, LANES), f32),
            *[pltpu.VMEM((CLON + 2, LEV, LANES), f32) for _ in range(STEPS + 1)],
            pltpu.VMEM((STEPS + 1, LEV, LANES), f32),
            pltpu.VMEM((STEPS, LEV, LANES), f32),
            pltpu.VMEM((STEPS, LEV, LANES), f32),
            pltpu.VMEM((2, LEV, LANES), f32),
            pltpu.VMEM((8, LANES), f32),
            pltpu.VMEM((8, LANES), jnp.int32),
            pltpu.VMEM((LEV, DEPTH), jnp.bfloat16),
            pltpu.SemaphoreType.DMA((CHIPS,)),
            pltpu.SemaphoreType.DMA,
            pltpu.SemaphoreType.DMA((DEVICES,)),
            pltpu.SemaphoreType.DMA((DEVICES,)),
            pltpu.SemaphoreType.DMA((4 * STEPS,)),
            pltpu.SemaphoreType.DMA((4 * STEPS,)),
        ],
        compiler_params=pltpu.CompilerParams(
            collective_id=0, has_side_effects=True, vmem_limit_bytes=44 * 2**20
        ),
    )(
        *(
            pltpu.with_memory_space_constraint(value, pltpu.HBM)
            for value in (
                kernels,
                weighted_residuals.reshape(CHIPS, LANES),
                sounding_columns.reshape(CHIPS, LANES),
                segment_counts,
                courant,
                mix_strength,
                cloud_top,
                redistribution,
            )
        )
    )
    return field.transpose(1, 0, 2), flux


def solution(mesh):
    return jax.shard_map(
        on_device,
        mesh=mesh,
        in_specs=(
            P(None, ("lon", "lat")),
            P(("lon", "lat")),
            P(("lon", "lat")),
            P(("lon", "lat"), None),
            P(None, None, "lon", "lat"),
            P("lon", "lat"),
            P("lon", "lat"),
            P(),
        ),
        out_specs=(P(None, "lon", "lat"), P("lon", "lat")),
        check_vma=False,
    )
```

```python
import itertools
import random

import jax
import jax.numpy as jnp
from jax import lax
from jax.experimental import pallas as pl
from jax.experimental.pallas import tpu as pltpu
from jax.sharding import PartitionSpec as P

STEPS = 4
LEV = 72
CLON = 48
LANES = 128
CHIPS = 64
DEVICES = 128
ROWS = 37
BLOCKS = 8
UNROLL = 6
PAIRS = 11
LAST = 4
DEPTH = 80

OFFSETS = list(itertools.product(range(4), repeat=3))
random.Random(1).shuffle(OFFSETS)
OFFSETS.sort(key=lambda o: sum(min(v, 4 - v) for v in o))
OFFSETS = OFFSETS[1:] + OFFSETS[:1]


def coords():
    lon = lax.axis_index("lon")
    lat = lax.axis_index("lat")
    return lon % 4, (lon // 4) % 4, (lat // 2) * 2 + lon // 16, lat % 2


def placer():
    x, y, z, c = coords()
    way = 1 + 2 * c
    xs = [lax.rem(x + d * way, 4) for d in range(4)]
    ys = [lax.rem(y + d * way, 4) * 4 for d in range(4)]
    zs = [lax.rem(z + d * way, 4) for d in range(4)]
    inner = [lax.rem(v, 2) * 16 for v in zs]
    outer = [lax.div(v, 2) * 2 for v in zs]
    cores = [c, 1 - c]

    def place(dx, dy, dz, dc):
        return inner[dz] + ys[dy] + xs[dx], outer[dz] + cores[dc]

    return place


def to(lon, lat):
    return {"lon": lon, "lat": lat}


def iota(shape, dim):
    return lax.broadcasted_iota(jnp.int32, shape, dim)


def split(value):
    high = value.astype(jnp.bfloat16).astype(jnp.float32)
    return high, value - high


def lanes(low, high):
    lane = iota((1, LANES), 1)
    return (lane == low) | (lane == high)


def pack_ends(i, value, field):
    return jnp.where(lanes(2 * i, 2 * i + 1), pltpu.roll(value, 2 * i + 1, 1), field)


def pack_near(i, value, field):
    return jnp.where(lanes(2 * i, 2 * i + 3), pltpu.roll(value, 2 * i + 2, 1), field)


def put_ends(i, field, value):
    ends = pltpu.roll(field, LANES - 1 - 2 * i, 1)
    return jnp.where(lanes(LANES - 1, 0), ends, value)


def spread_ends(field):
    even = lax.rem(iota((1, LANES), 1), 2) == 0
    return jnp.where(even, field, pltpu.roll(field, 2, 1))


def transport(x, east, west, north, south, a, b):
    along = jnp.where(a > 0, east, west)
    over = jnp.where(b > 0, north, south)
    return x + jnp.abs(a) * (along - x) + jnp.abs(b) * (over - x)


def convect(columns, mixer):
    sources, inside = [], []
    for field, top, strength in columns:
        inner = iota((LEV, LANES), 0) < top
        source = jnp.where(inner, field * strength, 0.0)
        pad = jnp.zeros((DEPTH - LEV, LANES), jnp.float32)
        source = jnp.concatenate([source, pad], axis=0)
        high = source.astype(jnp.bfloat16)
        rest = (source - high.astype(jnp.float32)).astype(jnp.bfloat16)
        sources.append(jnp.concatenate([high, rest, high], axis=0))
        inside.append(inner)
    stack = jnp.concatenate(sources, axis=1)
    mixed = jnp.dot(mixer, stack, preferred_element_type=jnp.float32)
    return [
        column[0] + jnp.where(inner, mixed[:, h * LANES : (h + 1) * LANES], 0.0)
        for h, (column, inner) in enumerate(zip(columns, inside))
    ]


def kernel(
    kernels,
    residuals_in,
    columns_in,
    counts_in,
    courant,
    strength_in,
    cloud_top_in,
    redistribution_in,
    out,
    flux,
    residuals,
    columns,
    counts,
    strength,
    cloud_top,
    redistribution,
    small_sem,
    forcing_in,
    wind,
    send,
    recv,
    state_0,
    state_1,
    state_2,
    state_3,
    state_4,
    edge,
    from_south,
    from_north,
    strip_wind,
    strip_strength,
    strip_top,
    mixer,
    spread,
    load_sem,
    wind_sem,
    send_sem,
    recv_sem,
    edge_send,
    edge_recv,
):
    states = (state_0, state_1, state_2, state_3, state_4)
    lon, lat = lax.axis_index("lon"), lax.axis_index("lat")
    core = lat % 2
    at_offset = placer()
    barrier = pltpu.get_barrier_semaphore()
    for offset in reversed(OFFSETS):
        for c in range(2):
            if any(offset) or c:
                pl.semaphore_signal(barrier, 1, device_id=to(*at_offset(*offset, c)))

    chips = [at_offset(*offset, 0) for offset in OFFSETS]
    chips = [there_lon * 2 + lax.div(there_lat, 2) for there_lon, there_lat in chips]

    def load(m):
        at = pl.ds(pl.multiple_of(chips[m] * LANES, LANES), LANES)
        return pltpu.make_async_copy(
            kernels.at[:, at], forcing_in.at[:, at], load_sem.at[m]
        )

    small = [
        pltpu.make_async_copy(source, target, small_sem.at[i])
        for i, (source, target) in enumerate(
            (
                (counts_in, counts),
                (residuals_in, residuals),
                (columns_in, columns),
                (strength_in, strength),
                (cloud_top_in, cloud_top),
                (redistribution_in, redistribution),
            )
        )
    ]
    for copy in small:
        copy.start()
    for m in range(CHIPS):
        load(m).start()
    def fetch(i, carry):
        for part in range(2):
            pltpu.make_async_copy(
                courant.at[part, :, i, :], wind.at[part, i], wind_sem
            ).start()
        return carry


    lane = iota((8, LANES), 1)
    sub = iota((8, LANES), 0)
    low = lane < 64

    def lo_half(shape):
        return iota(shape, 1) < 64

    def block_copy(k, there):
        return pltpu.make_async_remote_copy(
            src_ref=send.at[k],
            dst_ref=recv.at[k],
            send_sem=send_sem.at[k],
            recv_sem=recv_sem.at[k],
            device_id=to(*there),
        )

    mine = DEVICES - 2

    def send_to(m):
        load(m).wait()
        chip = chips[m]
        one = counts[0, 2 * chip]
        two = counts[0, 2 * chip + 1]
        row = iota((1, LANES), 1)
        live = (row % 64) < jnp.where(row < 64, one, two)
        weight = jnp.where(live, residuals[pl.ds(chip, 1), :], 0.0)
        place = columns[pl.ds(chip, 1), :].astype(jnp.float32)
        start = pl.multiple_of(chip * LANES, LANES)
        value = forcing_in[:, pl.ds(start, LANES)] * weight
        a, b, last = value[0:32], value[32:64], value[64:72]
        half = lo_half((32, LANES))
        turned = pltpu.roll(last, 4, 0)
        tail_0 = jnp.where(low, last, pltpu.roll(turned, 64, 1))
        tail_1 = jnp.where(low, pltpu.roll(last, 64, 1), turned)
        place_8 = jnp.broadcast_to(place, (8, LANES))
        tail_0 = jnp.where(sub == 4, place_8, tail_0)
        tail_1 = jnp.where(sub == 4, pltpu.roll(place_8, 64, 1), tail_1)
        slot_0 = 2 * m + core
        slot_1 = 2 * m + 1 - core
        send[slot_0, 0:32, :] = jnp.where(half, a, pltpu.roll(b, 64, 1))
        send[slot_1, 0:32, :] = jnp.where(half, pltpu.roll(a, 64, 1), b)
        send[slot_0, 32:ROWS, :] = tail_0[0:5]
        send[slot_1, 32:ROWS, :] = tail_1[0:5]
        for c in range(2):
            if 2 * m + c != mine:
                block_copy(2 * m + c, at_offset(*OFFSETS[m], c)).start()
            else:
                recv[mine] = send[mine]

    for copy in small:
        copy.wait()
    pl.semaphore_wait(barrier, DEVICES - 1)
    for m in range(CHIPS):
        send_to(m)
    lax.fori_loop(0, CLON, fetch, 0)

    high, rest = split(redistribution[...].T)
    pad = jnp.zeros((LEV, DEPTH - LEV), jnp.float32)
    mixer[...] = jnp.concatenate([high, pad, high, pad, rest, pad], axis=1).astype(
        jnp.bfloat16
    )

    def clear(i, carry):
        state_0[i] = jnp.zeros((LEV, LANES), jnp.float32)
        return carry

    lax.fori_loop(1, CLON + 1, clear, 0)

    pltpu.make_async_copy(wind, wind, wind_sem).wait()
    nothing = jnp.zeros((LEV, LANES), jnp.float32)
    few = jnp.zeros((8, LANES), jnp.float32)

    def pack_static(g, fields):
        a, b, c, d = fields
        for k in range(UNROLL):
            i = g * UNROLL + k
            a = pack_ends(i, wind[0, i], a)
            b = pack_ends(i, wind[1, i], b)
            row = strength[pl.ds(i, 1), :]
            c = pack_ends(i, jnp.broadcast_to(row, (8, LANES)), c)
            row = cloud_top[pl.ds(i, 1), :].astype(jnp.float32)
            d = pack_ends(i, jnp.broadcast_to(row, (8, LANES)), d)
        return a, b, c, d

    strips = lax.fori_loop(0, CLON // UNROLL, pack_static, (nothing, nothing, few, few))
    strip_wind[0], strip_wind[1], strip_strength[...] = strips[:3]
    strip_top[...] = strips[3].astype(jnp.int32)

    def paired(k):
        half = lo_half((32, LANES))
        one, two = recv[k, 0:32, :], recv[k + 1, 0:32, :]
        end_1, end_2 = recv[k, 29:ROWS, :], recv[k + 1, 29:ROWS, :]
        top = jnp.where(half, one, pltpu.roll(two, 64, 1))
        bottom = jnp.where(half, pltpu.roll(one, 64, 1), two)
        end_top = jnp.where(low, end_1, pltpu.roll(end_2, 64, 1))
        end_bottom = jnp.where(low, pltpu.roll(end_1, 64, 1), end_2)
        end = jnp.where(sub < 4, pltpu.roll(end_top, 5, 0), pltpu.roll(end_bottom, 1, 0))
        return jnp.concatenate([top, bottom, end], axis=0), end_top[7:8]

    def gather(first, blocks):
        values, places = [], []
        for i in range(blocks):
            if not isinstance(first, int) or first + i != mine:
                block_copy(first + i, (lon, lat)).wait_recv()
        for i in range(0, blocks, 2):
            value, place = paired(first + i)
            high, rest = split(value)
            values.append(jnp.concatenate([high, rest], axis=0))
            places.append(place)
        both = jnp.concatenate(values, axis=1).astype(jnp.bfloat16)
        place = jnp.concatenate(places, axis=1).astype(jnp.int32)
        across = lax.div(place, 256)
        within = lax.rem(place, 256)
        hot = iota((256, blocks * 64), 0) == within
        hot = jnp.where(hot, 1.0, 0.0).astype(jnp.bfloat16)
        for q in range(0, CLON // 2, 2):
            masks = [
                jnp.where(across == q + h, 1.0, 0.0).astype(jnp.bfloat16) for h in range(2)
            ]
            put = lax.dot_general(
                jnp.concatenate([both * mask for mask in masks], axis=0),
                hot,
                (((1,), (1,)), ((), ())),
                preferred_element_type=jnp.float32,
            )
            for h in range(2):
                part = put[2 * h * LEV : (2 * h + 1) * LEV]
                part = part + put[(2 * h + 1) * LEV : (2 * h + 2) * LEV]
                state_0[2 * (q + h) + 1] += part[:, :LANES]
                state_0[2 * (q + h) + 2] += part[:, LANES:]

    def gather_step(t, carry):
        gather(BLOCKS * t, BLOCKS)
        return carry

    lax.fori_loop(0, DEVICES // BLOCKS - 1, gather_step, 0)
    for first in range(DEVICES - BLOCKS, DEVICES, LAST):
        gather(first, LAST)

    east, west = lax.rem(lon + 1, 32), lax.rem(lon + 31, 32)
    north, south = lax.rem(lat + 1, 4), lax.rem(lat + 3, 4)

    def edge_copies(s, which=range(4)):
        parts = (
            (states[s].at[1], states[s].at[CLON + 1], (west, lat)),
            (states[s].at[CLON], states[s].at[0], (east, lat)),
            (edge.at[s], from_south.at[s], (lon, north)),
            (edge.at[s], from_north.at[s], (lon, south)),
        )
        return [
            pltpu.make_async_remote_copy(
                src_ref=source,
                dst_ref=target,
                send_sem=edge_send.at[4 * s + i],
                recv_sem=edge_recv.at[4 * s + i],
                device_id=to(*there),
            )
            for i, (source, target, there) in enumerate(parts)
            if i in which
        ]

    for copy in edge_copies(0, range(2)):
        copy.start()

    def pack_first(g, fields):
        ends, near = fields
        for k in range(UNROLL):
            i = g * UNROLL + k
            value = state_0[i + 1]
            ends, near = pack_ends(i, value, ends), pack_near(i, value, near)
        return ends, near

    first = lax.fori_loop(0, CLON // UNROLL, pack_first, (nothing, nothing))
    edge[0], near = first
    flux[...] = jnp.zeros((CLON, LANES), jnp.float32)
    flux_ends = few

    lane_row = iota((1, LANES), 1)
    even = lax.rem(lane_row, 2) == 0

    for s in range(STEPS):
        now, later = states[s], states[s + 1]
        for copy in edge_copies(s, range(0 if s else 2, 4)):
            copy.start()

        def row(i, whole):
            x = now[i + 1]
            after, before = pltpu.roll(x, LANES - 1, 1), pltpu.roll(x, 1, 1)
            if not whole:
                ends = pltpu.roll(spread[...], LANES - 2 - 2 * i, 1)
                after = jnp.where(lane_row == LANES - 2, ends, after)
                before = jnp.where(lane_row == 1, ends, before)
            moved = transport(
                x, now[i + 2], now[i], after, before, wind[0, i], wind[1, i]
            )
            return moved, cloud_top[pl.ds(i, 1), :], strength[pl.ds(i, 1), :]

        def advance_pair(i, field):
            values = convect([row(i, s == 0), row(i + 1, s == 0)], mixer[...])
            for h, value in enumerate(values):
                later[i + h + 1] = value
                flux[pl.ds(i + h, 1), :] += value[0:1]
                field = pack_near(i + h, value, field)
            return field

        def advance(g, field):
            for k in range(PAIRS):
                field = advance_pair(1 + 2 * (g * PAIRS + k), field)
            return field

        groups = (CLON - 2) // 2 // PAIRS
        next_near = lax.fori_loop(0, groups, advance, nothing)
        for i in range(1 + 2 * groups * PAIRS, CLON - 1, 2):
            next_near = advance_pair(i, next_near)

        for copy in edge_copies(s):
            copy.wait_recv()
        x = edge[s]
        near = jnp.where(even, near, pltpu.roll(near, LANES - 2, 1))
        above = jnp.where(lat < 3, from_north[s], 0.0)
        below = jnp.where(lat > 0, from_south[s], 0.0)
        after = jnp.where(even, pltpu.roll(above, LANES - 1, 1), near)
        before = jnp.where(even, near, pltpu.roll(below, 1, 1))
        around = pack_ends(CLON, now[CLON + 1], pack_ends(63, now[0], x))
        moved = transport(
            x,
            pltpu.roll(around, LANES - 2, 1),
            pltpu.roll(around, 2, 1),
            after,
            before,
            strip_wind[0],
            strip_wind[1],
        )
        strip = (moved, strip_top[0:1, :], strip_strength[0:1, :])
        ends, one, two = convect([strip, row(0, True), row(CLON - 1, True)], mixer[...])
        edge[s + 1] = ends
        spread[...] = spread_ends(ends)
        flux_ends = flux_ends + ends[0:8]
        for i, value in ((0, one), (CLON - 1, two)):
            later[i + 1] = put_ends(i, ends, value)
            flux[pl.ds(i, 1), :] += value[0:1]
            next_near = pack_near(i, value, next_near)
        near = next_near

    def finish(g, carry):
        for k in range(UNROLL):
            i = g * UNROLL + k
            out[i] = put_ends(i, edge[STEPS], state_4[i + 1])
            total = jnp.broadcast_to(flux[pl.ds(i, 1), :], (8, LANES))
            flux[pl.ds(i, 1), :] = put_ends(i, flux_ends, total)[0:1]
        return carry

    lax.fori_loop(0, CLON // UNROLL, finish, 0)

    def sent(k, carry):
        block_copy(k, (lon, lat)).wait_send()
        return carry

    lax.fori_loop(0, mine, sent, 0)
    block_copy(DEVICES - 1, (lon, lat)).wait_send()
    for s in range(STEPS):
        for copy in edge_copies(s):
            copy.wait_send()


def on_device(
    kernels,
    weighted_residuals,
    sounding_columns,
    segment_counts,
    courant,
    mix_strength,
    cloud_top,
    redistribution,
):
    in_vmem = pl.BlockSpec(memory_space=pltpu.VMEM)
    f32 = jnp.float32
    field, flux = pl.pallas_call(
        kernel,
        out_shape=(
            pltpu.VMEM((CLON, LEV, LANES), f32),
            pltpu.VMEM((CLON, LANES), f32),
        ),
        in_specs=[pl.BlockSpec(memory_space=pl.ANY)] * 8,
        out_specs=(in_vmem, in_vmem),
        scratch_shapes=[
            pltpu.VMEM((CHIPS, LANES), f32),
            pltpu.VMEM((CHIPS, LANES), jnp.int32),
            pltpu.SMEM((1, DEVICES), jnp.int32),
            pltpu.VMEM((CLON, LANES), f32),
            pltpu.VMEM((CLON, LANES), jnp.int32),
            pltpu.VMEM((LEV, LEV), f32),
            pltpu.SemaphoreType.DMA((6,)),
            pltpu.VMEM((LEV, CHIPS * LANES), f32),
            pltpu.VMEM((2, CLON, LEV, LANES), f32),
            pltpu.VMEM((DEVICES, ROWS, LANES), f32),
            pltpu.VMEM((DEVICES, ROWS, LANES), f32),
            *[pltpu.VMEM((CLON + 2, LEV, LANES), f32) for _ in range(STEPS + 1)],
            pltpu.VMEM((STEPS + 1, LEV, LANES), f32),
            pltpu.VMEM((STEPS, LEV, LANES), f32),
            pltpu.VMEM((STEPS, LEV, LANES), f32),
            pltpu.VMEM((2, LEV, LANES), f32),
            pltpu.VMEM((8, LANES), f32),
            pltpu.VMEM((8, LANES), jnp.int32),
            pltpu.VMEM((LEV, 3 * DEPTH), jnp.bfloat16),
            pltpu.VMEM((LEV, LANES), f32),
            pltpu.SemaphoreType.DMA((CHIPS,)),
            pltpu.SemaphoreType.DMA,
            pltpu.SemaphoreType.DMA((DEVICES,)),
            pltpu.SemaphoreType.DMA((DEVICES,)),
            pltpu.SemaphoreType.DMA((4 * STEPS,)),
            pltpu.SemaphoreType.DMA((4 * STEPS,)),
        ],
        compiler_params=pltpu.CompilerParams(
            collective_id=0, has_side_effects=True, vmem_limit_bytes=44 * 2**20
        ),
    )(
        *(
            pltpu.with_memory_space_constraint(value, pltpu.HBM)
            for value in (
                kernels,
                weighted_residuals.reshape(CHIPS, LANES),
                sounding_columns.reshape(CHIPS, LANES),
                segment_counts,
                courant,
                mix_strength,
                cloud_top,
                redistribution,
            )
        )
    )
    return field.transpose(1, 0, 2), flux


def solution(mesh):
    return jax.shard_map(
        on_device,
        mesh=mesh,
        in_specs=(
            P(None, ("lon", "lat")),
            P(("lon", "lat")),
            P(("lon", "lat")),
            P(("lon", "lat"), None),
            P(None, None, "lon", "lat"),
            P("lon", "lat"),
            P("lon", "lat"),
            P(),
        ),
        out_specs=(P(None, "lon", "lat"), P("lon", "lat")),
        check_vma=False,
    )
```

```python
import itertools
import random

import jax
import jax.numpy as jnp
from jax import lax
from jax.experimental import pallas as pl
from jax.experimental.pallas import tpu as pltpu
from jax.sharding import PartitionSpec as P

STEPS = 4
LEV = 72
CLON = 48
LANES = 128
CHIPS = 64
DEVICES = 128
ROWS = 37
BLOCKS = 8
UNROLL = 6
PAIRS = 11
LAST = 4
DEPTH = 80

OFFSETS = list(itertools.product(range(4), repeat=3))
random.Random(1).shuffle(OFFSETS)
OFFSETS.sort(key=lambda o: sum(min(v, 4 - v) for v in o))
OFFSETS = OFFSETS[1:] + OFFSETS[:1]


def coords():
    lon = lax.axis_index("lon")
    lat = lax.axis_index("lat")
    return lon % 4, (lon // 4) % 4, (lat // 2) * 2 + lon // 16, lat % 2


def placer():
    x, y, z, c = coords()
    way = 1 + 2 * c
    xs = [lax.rem(x + d * way, 4) for d in range(4)]
    ys = [lax.rem(y + d * way, 4) * 4 for d in range(4)]
    zs = [lax.rem(z + d * way, 4) for d in range(4)]
    inner = [lax.rem(v, 2) * 16 for v in zs]
    outer = [lax.div(v, 2) * 2 for v in zs]
    cores = [c, 1 - c]

    def place(dx, dy, dz, dc):
        return inner[dz] + ys[dy] + xs[dx], outer[dz] + cores[dc]

    return place


def to(lon, lat):
    return {"lon": lon, "lat": lat}


def iota(shape, dim):
    return lax.broadcasted_iota(jnp.int32, shape, dim)


def split(value):
    high = value.astype(jnp.bfloat16).astype(jnp.float32)
    return high, value - high


def lanes(low, high):
    lane = iota((1, LANES), 1)
    return (lane == low) | (lane == high)


def pack_ends(i, value, field):
    return jnp.where(lanes(2 * i, 2 * i + 1), pltpu.roll(value, 2 * i + 1, 1), field)


def pack_near(i, value, field):
    return jnp.where(lanes(2 * i, 2 * i + 3), pltpu.roll(value, 2 * i + 2, 1), field)


def put_ends(i, field, value):
    ends = pltpu.roll(field, LANES - 1 - 2 * i, 1)
    return jnp.where(lanes(LANES - 1, 0), ends, value)


def spread_ends(field):
    even = lax.rem(iota((1, LANES), 1), 2) == 0
    return jnp.where(even, field, pltpu.roll(field, 2, 1))


def transport(x, east, west, north, south, a, b):
    along = jnp.where(a > 0, east, west)
    over = jnp.where(b > 0, north, south)
    return x + jnp.abs(a) * (along - x) + jnp.abs(b) * (over - x)


def convect(columns, mixer):
    sources, inside = [], []
    for field, top, strength in columns:
        inner = iota((LEV, LANES), 0) < top
        source = jnp.where(inner, field * strength, 0.0)
        pad = jnp.zeros((DEPTH - LEV, LANES), jnp.float32)
        source = jnp.concatenate([source, pad], axis=0)
        high = source.astype(jnp.bfloat16)
        rest = (source - high.astype(jnp.float32)).astype(jnp.bfloat16)
        sources.append(jnp.concatenate([high, rest, high], axis=0))
        inside.append(inner)
    stack = jnp.concatenate(sources, axis=1)
    mixed = jnp.dot(mixer, stack, preferred_element_type=jnp.float32)
    return [
        column[0] + jnp.where(inner, mixed[:, h * LANES : (h + 1) * LANES], 0.0)
        for h, (column, inner) in enumerate(zip(columns, inside))
    ]


def kernel(
    kernels,
    residuals_in,
    columns_in,
    counts_in,
    courant,
    strength_in,
    cloud_top_in,
    redistribution_in,
    out,
    out_ends,
    flux,
    flux_ends,
    residuals,
    columns,
    counts,
    strength,
    cloud_top,
    redistribution,
    small_sem,
    forcing_in,
    wind,
    send,
    recv,
    state_0,
    state_1,
    state_2,
    state_3,
    edge,
    from_south,
    from_north,
    strip_wind,
    strip_strength,
    strip_top,
    mixer,
    spread,
    load_sem,
    wind_sem,
    send_sem,
    recv_sem,
    edge_send,
    edge_recv,
):
    states = (state_0, state_1, state_2, state_3)
    lon, lat = lax.axis_index("lon"), lax.axis_index("lat")
    core = lat % 2
    at_offset = placer()
    barrier = pltpu.get_barrier_semaphore()
    for offset in reversed(OFFSETS):
        for c in range(2):
            if any(offset) or c:
                pl.semaphore_signal(barrier, 1, device_id=to(*at_offset(*offset, c)))

    chips = [at_offset(*offset, 0) for offset in OFFSETS]
    chips = [there_lon * 2 + lax.div(there_lat, 2) for there_lon, there_lat in chips]

    def load(m):
        at = pl.ds(pl.multiple_of(chips[m] * LANES, LANES), LANES)
        return pltpu.make_async_copy(
            kernels.at[:, at], forcing_in.at[:, at], load_sem.at[m]
        )

    small = [
        pltpu.make_async_copy(source, target, small_sem.at[i])
        for i, (source, target) in enumerate(
            (
                (counts_in, counts),
                (residuals_in, residuals),
                (columns_in, columns),
                (strength_in, strength),
                (cloud_top_in, cloud_top),
                (redistribution_in, redistribution),
            )
        )
    ]
    for copy in small:
        copy.start()
    for m in range(CHIPS):
        load(m).start()
    def fetch(i, carry):
        for part in range(2):
            pltpu.make_async_copy(
                courant.at[part, :, i, :], wind.at[part, i], wind_sem
            ).start()
        return carry


    lane = iota((8, LANES), 1)
    sub = iota((8, LANES), 0)
    low = lane < 64

    def lo_half(shape):
        return iota(shape, 1) < 64

    def block_copy(k, there):
        return pltpu.make_async_remote_copy(
            src_ref=send.at[k],
            dst_ref=recv.at[k],
            send_sem=send_sem.at[k],
            recv_sem=recv_sem.at[k],
            device_id=to(*there),
        )

    mine = DEVICES - 2

    def send_to(m):
        load(m).wait()
        chip = chips[m]
        one = counts[0, 2 * chip]
        two = counts[0, 2 * chip + 1]
        row = iota((1, LANES), 1)
        live = (row % 64) < jnp.where(row < 64, one, two)
        weight = jnp.where(live, residuals[pl.ds(chip, 1), :], 0.0)
        place = columns[pl.ds(chip, 1), :].astype(jnp.float32)
        start = pl.multiple_of(chip * LANES, LANES)
        value = forcing_in[:, pl.ds(start, LANES)] * weight
        a, b, last = value[0:32], value[32:64], value[64:72]
        half = lo_half((32, LANES))
        turned = pltpu.roll(last, 4, 0)
        tail_0 = jnp.where(low, last, pltpu.roll(turned, 64, 1))
        tail_1 = jnp.where(low, pltpu.roll(last, 64, 1), turned)
        place_8 = jnp.broadcast_to(place, (8, LANES))
        tail_0 = jnp.where(sub == 4, place_8, tail_0)
        tail_1 = jnp.where(sub == 4, pltpu.roll(place_8, 64, 1), tail_1)
        slot_0 = 2 * m + core
        slot_1 = 2 * m + 1 - core
        send[slot_0, 0:32, :] = jnp.where(half, a, pltpu.roll(b, 64, 1))
        send[slot_1, 0:32, :] = jnp.where(half, pltpu.roll(a, 64, 1), b)
        send[slot_0, 32:ROWS, :] = tail_0[0:5]
        send[slot_1, 32:ROWS, :] = tail_1[0:5]
        for c in range(2):
            if 2 * m + c != mine:
                block_copy(2 * m + c, at_offset(*OFFSETS[m], c)).start()
            else:
                recv[mine] = send[mine]

    for copy in small:
        copy.wait()
    pl.semaphore_wait(barrier, DEVICES - 1)
    for m in range(CHIPS):
        send_to(m)
    lax.fori_loop(0, CLON, fetch, 0)

    high, rest = split(redistribution[...].T)
    pad = jnp.zeros((LEV, DEPTH - LEV), jnp.float32)
    mixer[...] = jnp.concatenate([high, pad, high, pad, rest, pad], axis=1).astype(
        jnp.bfloat16
    )

    def clear(i, carry):
        state_0[i] = jnp.zeros((LEV, LANES), jnp.float32)
        return carry

    lax.fori_loop(1, CLON + 1, clear, 0)

    pltpu.make_async_copy(wind, wind, wind_sem).wait()
    nothing = jnp.zeros((LEV, LANES), jnp.float32)
    few = jnp.zeros((8, LANES), jnp.float32)

    def pack_static(g, fields):
        a, b, c, d = fields
        for k in range(UNROLL):
            i = g * UNROLL + k
            a = pack_ends(i, wind[0, i], a)
            b = pack_ends(i, wind[1, i], b)
            row = strength[pl.ds(i, 1), :]
            c = pack_ends(i, jnp.broadcast_to(row, (8, LANES)), c)
            row = cloud_top[pl.ds(i, 1), :].astype(jnp.float32)
            d = pack_ends(i, jnp.broadcast_to(row, (8, LANES)), d)
        return a, b, c, d

    strips = lax.fori_loop(0, CLON // UNROLL, pack_static, (nothing, nothing, few, few))
    strip_wind[0], strip_wind[1], strip_strength[...] = strips[:3]
    strip_top[...] = strips[3].astype(jnp.int32)

    def paired(k):
        half = lo_half((32, LANES))
        one, two = recv[k, 0:32, :], recv[k + 1, 0:32, :]
        end_1, end_2 = recv[k, 29:ROWS, :], recv[k + 1, 29:ROWS, :]
        top = jnp.where(half, one, pltpu.roll(two, 64, 1))
        bottom = jnp.where(half, pltpu.roll(one, 64, 1), two)
        end_top = jnp.where(low, end_1, pltpu.roll(end_2, 64, 1))
        end_bottom = jnp.where(low, pltpu.roll(end_1, 64, 1), end_2)
        end = jnp.where(sub < 4, pltpu.roll(end_top, 5, 0), pltpu.roll(end_bottom, 1, 0))
        return jnp.concatenate([top, bottom, end], axis=0), end_top[7:8]

    def gather(first, blocks):
        values, places = [], []
        for i in range(blocks):
            if not isinstance(first, int) or first + i != mine:
                block_copy(first + i, (lon, lat)).wait_recv()
        for i in range(0, blocks, 2):
            value, place = paired(first + i)
            high, rest = split(value)
            values.append(jnp.concatenate([high, rest], axis=0))
            places.append(place)
        both = jnp.concatenate(values, axis=1).astype(jnp.bfloat16)
        place = jnp.concatenate(places, axis=1).astype(jnp.int32)
        across = lax.div(place, 256)
        within = lax.rem(place, 256)
        hot = iota((256, blocks * 64), 0) == within
        hot = jnp.where(hot, 1.0, 0.0).astype(jnp.bfloat16)
        for q in range(0, CLON // 2, 2):
            masks = [
                jnp.where(across == q + h, 1.0, 0.0).astype(jnp.bfloat16) for h in range(2)
            ]
            put = lax.dot_general(
                jnp.concatenate([both * mask for mask in masks], axis=0),
                hot,
                (((1,), (1,)), ((), ())),
                preferred_element_type=jnp.float32,
            )
            for h in range(2):
                part = put[2 * h * LEV : (2 * h + 1) * LEV]
                part = part + put[(2 * h + 1) * LEV : (2 * h + 2) * LEV]
                state_0[2 * (q + h) + 1] += part[:, :LANES]
                state_0[2 * (q + h) + 2] += part[:, LANES:]

    def gather_step(t, carry):
        gather(BLOCKS * t, BLOCKS)
        return carry

    lax.fori_loop(0, DEVICES // BLOCKS - 1, gather_step, 0)
    for first in range(DEVICES - BLOCKS, DEVICES, LAST):
        gather(first, LAST)

    east, west = lax.rem(lon + 1, 32), lax.rem(lon + 31, 32)
    north, south = lax.rem(lat + 1, 4), lax.rem(lat + 3, 4)

    def edge_copies(s, which=range(4)):
        parts = (
            (states[s].at[1], states[s].at[CLON + 1], (west, lat)),
            (states[s].at[CLON], states[s].at[0], (east, lat)),
            (edge.at[s], from_south.at[s], (lon, north)),
            (edge.at[s], from_north.at[s], (lon, south)),
        )
        return [
            pltpu.make_async_remote_copy(
                src_ref=source,
                dst_ref=target,
                send_sem=edge_send.at[4 * s + i],
                recv_sem=edge_recv.at[4 * s + i],
                device_id=to(*there),
            )
            for i, (source, target, there) in enumerate(parts)
            if i in which
        ]

    for copy in edge_copies(0, range(2)):
        copy.start()

    def pack_first(g, fields):
        ends, near = fields
        for k in range(UNROLL):
            i = g * UNROLL + k
            value = state_0[i + 1]
            ends, near = pack_ends(i, value, ends), pack_near(i, value, near)
        return ends, near

    first = lax.fori_loop(0, CLON // UNROLL, pack_first, (nothing, nothing))
    edge[0], near = first
    for copy in edge_copies(0, range(2, 4)):
        copy.start()
    flux[...] = jnp.zeros((CLON, LANES), jnp.float32)
    flux_ends[...] = few

    lane_row = iota((1, LANES), 1)
    even = lax.rem(lane_row, 2) == 0

    for s in range(STEPS):
        now = states[s]
        last = s + 1 == STEPS
        later = out if last else states[s + 1]
        shift = 0 if last else 1

        def row(i, halos=None):
            x, west, east = now[i + 1], now[i], now[i + 2]
            after, before = pltpu.roll(x, LANES - 1, 1), pltpu.roll(x, 1, 1)
            if halos:
                above, below = halos
                if i:
                    west = put_ends(i - 1, edge[s], west)
                else:
                    east = put_ends(i + 1, edge[s], east)
                above = pltpu.roll(above, LANES - 2 - 2 * i, 1)
                below = pltpu.roll(below, (LANES - 2 * i) % LANES, 1)
                after = jnp.where(lane_row == LANES - 1, above, after)
                before = jnp.where(lane_row == 0, below, before)
            elif s:
                ends = pltpu.roll(spread[...], LANES - 2 - 2 * i, 1)
                after = jnp.where(lane_row == LANES - 2, ends, after)
                before = jnp.where(lane_row == 1, ends, before)
            moved = transport(x, east, west, after, before, wind[0, i], wind[1, i])
            return moved, cloud_top[pl.ds(i, 1), :], strength[pl.ds(i, 1), :]

        def advance_pair(i, field):
            values = convect([row(i), row(i + 1)], mixer[...])
            for h, value in enumerate(values):
                later[i + h + shift] = value
                flux[pl.ds(i + h, 1), :] += value[0:1]
                if not last:
                    field = pack_near(i + h, value, field)
            return field

        def advance(g, field):
            for k in range(PAIRS):
                field = advance_pair(1 + 2 * (g * PAIRS + k), field)
            return field

        groups = (CLON - 2) // 2 // PAIRS
        next_near = lax.fori_loop(0, groups, advance, nothing)
        for i in range(1 + 2 * groups * PAIRS, CLON - 1, 2):
            next_near = advance_pair(i, next_near)

        x = edge[s]
        near = jnp.where(even, near, pltpu.roll(near, LANES - 2, 1))
        east_of, west_of = pltpu.roll(x, LANES - 2, 1), pltpu.roll(x, 2, 1)
        for copy in edge_copies(s):
            copy.wait_recv()
        above = jnp.where(lat < 3, from_north[s], 0.0)
        below = jnp.where(lat > 0, from_south[s], 0.0)
        borders = (0, CLON - 1)
        values = convect([row(i, (above, below)) for i in borders], mixer[...])
        for i, value in zip(borders, values):
            later[i + shift] = value
        if not last:
            for copy in edge_copies(s + 1, range(2)):
                copy.start()
        moved = transport(
            x,
            pack_ends(CLON - 1, now[CLON + 1], east_of),
            pack_ends(0, now[0], west_of),
            jnp.where(even, pltpu.roll(above, LANES - 1, 1), near),
            jnp.where(even, near, pltpu.roll(below, 1, 1)),
            strip_wind[0],
            strip_wind[1],
        )
        strip = (moved, strip_top[0:1, :], strip_strength[0:1, :])
        (ends,) = convect([strip], mixer[...])
        flux_ends[...] += ends[0:8]
        if last:
            out_ends[...] = ends
        else:
            edge[s + 1] = ends
            for copy in edge_copies(s + 1, range(2, 4)):
                copy.start()
            spread[...] = spread_ends(ends)
        for i, value in zip(borders, values):
            flux[pl.ds(i, 1), :] += value[0:1]
            if not last:
                next_near = pack_near(i, value, next_near)
        near = next_near

    def sent(k, carry):
        block_copy(k, (lon, lat)).wait_send()
        return carry

    lax.fori_loop(0, mine, sent, 0)
    block_copy(DEVICES - 1, (lon, lat)).wait_send()
    for s in range(STEPS):
        for copy in edge_copies(s):
            copy.wait_send()


def finish(field, ends, flux_in, flux_ends, out, flux, whole, whole_flux, sem, flux_sem):
    def group(g, carry):
        for k in range(UNROLL):
            i = g * UNROLL + k
            whole[i] = put_ends(i, ends[...], field[i])
            pltpu.make_async_copy(whole.at[i], out.at[:, i, :], sem).start()
            total = jnp.broadcast_to(flux_in[pl.ds(i, 1), :], (8, LANES))
            whole_flux[pl.ds(i, 1), :] = put_ends(i, flux_ends[...], total)[0:1]
        return carry

    lax.fori_loop(0, CLON // UNROLL, group, 0)
    last = pltpu.make_async_copy(whole_flux, flux, flux_sem)
    last.start()
    pltpu.make_async_copy(out, out, sem).wait()
    last.wait()


def on_device(
    kernels,
    weighted_residuals,
    sounding_columns,
    segment_counts,
    courant,
    mix_strength,
    cloud_top,
    redistribution,
):
    in_vmem = pl.BlockSpec(memory_space=pltpu.VMEM)
    f32 = jnp.float32
    parts = pl.pallas_call(
        kernel,
        out_shape=(
            pltpu.VMEM((CLON, LEV, LANES), f32),
            pltpu.VMEM((LEV, LANES), f32),
            pltpu.VMEM((CLON, LANES), f32),
            pltpu.VMEM((8, LANES), f32),
        ),
        in_specs=[pl.BlockSpec(memory_space=pl.ANY)] * 8,
        out_specs=(in_vmem,) * 4,
        scratch_shapes=[
            pltpu.VMEM((CHIPS, LANES), f32),
            pltpu.VMEM((CHIPS, LANES), jnp.int32),
            pltpu.SMEM((1, DEVICES), jnp.int32),
            pltpu.VMEM((CLON, LANES), f32),
            pltpu.VMEM((CLON, LANES), jnp.int32),
            pltpu.VMEM((LEV, LEV), f32),
            pltpu.SemaphoreType.DMA((6,)),
            pltpu.VMEM((LEV, CHIPS * LANES), f32),
            pltpu.VMEM((2, CLON, LEV, LANES), f32),
            pltpu.VMEM((DEVICES, ROWS, LANES), f32),
            pltpu.VMEM((DEVICES, ROWS, LANES), f32),
            *[pltpu.VMEM((CLON + 2, LEV, LANES), f32) for _ in range(STEPS)],
            pltpu.VMEM((STEPS, LEV, LANES), f32),
            pltpu.VMEM((STEPS, LEV, LANES), f32),
            pltpu.VMEM((STEPS, LEV, LANES), f32),
            pltpu.VMEM((2, LEV, LANES), f32),
            pltpu.VMEM((8, LANES), f32),
            pltpu.VMEM((8, LANES), jnp.int32),
            pltpu.VMEM((LEV, 3 * DEPTH), jnp.bfloat16),
            pltpu.VMEM((LEV, LANES), f32),
            pltpu.SemaphoreType.DMA((CHIPS,)),
            pltpu.SemaphoreType.DMA,
            pltpu.SemaphoreType.DMA((DEVICES,)),
            pltpu.SemaphoreType.DMA((DEVICES,)),
            pltpu.SemaphoreType.DMA((4 * STEPS,)),
            pltpu.SemaphoreType.DMA((4 * STEPS,)),
        ],
        compiler_params=pltpu.CompilerParams(
            collective_id=0, has_side_effects=True, vmem_limit_bytes=44 * 2**20
        ),
    )(
        *(
            pltpu.with_memory_space_constraint(value, pltpu.HBM)
            for value in (
                kernels,
                weighted_residuals.reshape(CHIPS, LANES),
                sounding_columns.reshape(CHIPS, LANES),
                segment_counts,
                courant,
                mix_strength,
                cloud_top,
                redistribution,
            )
        )
    )
    return pl.pallas_call(
        finish,
        out_shape=(
            jax.ShapeDtypeStruct((LEV, CLON, LANES), f32),
            jax.ShapeDtypeStruct((CLON, LANES), f32),
        ),
        in_specs=[in_vmem] * 4,
        out_specs=(pl.BlockSpec(memory_space=pl.ANY),) * 2,
        scratch_shapes=[
            pltpu.VMEM((CLON, LEV, LANES), f32),
            pltpu.VMEM((CLON, LANES), f32),
            pltpu.SemaphoreType.DMA,
            pltpu.SemaphoreType.DMA,
        ],
        compiler_params=pltpu.CompilerParams(vmem_limit_bytes=16 * 2**20),
    )(*parts)


def solution(mesh):
    return jax.shard_map(
        on_device,
        mesh=mesh,
        in_specs=(
            P(None, ("lon", "lat")),
            P(("lon", "lat")),
            P(("lon", "lat")),
            P(("lon", "lat"), None),
            P(None, None, "lon", "lat"),
            P("lon", "lat"),
            P("lon", "lat"),
            P(),
        ),
        out_specs=(P(None, "lon", "lat"), P("lon", "lat")),
        check_vma=False,
    )
```

```python
import itertools
import random

import jax
import jax.numpy as jnp
from jax import lax
from jax.experimental import pallas as pl
from jax.experimental.pallas import tpu as pltpu
from jax.sharding import PartitionSpec as P

STEPS = 4
LEV = 72
CLON = 48
LANES = 128
CHIPS = 64
DEVICES = 128
ROWS = 37
BLOCKS = 8
UNROLL = 12
PAIRS = 11
LAST = 8
DEPTH = 80

OFFSETS = list(itertools.product(range(4), repeat=3))
random.Random(1).shuffle(OFFSETS)
JITTER = random.Random(1)
OFFSETS.sort(key=lambda o: sum(min(v, 4 - v) for v in o) + JITTER.random() * 1.5)
OFFSETS.remove((0, 0, 0))
OFFSETS.append((0, 0, 0))


def coords():
    lon = lax.axis_index("lon")
    lat = lax.axis_index("lat")
    return lon % 4, (lon // 4) % 4, (lat // 2) * 2 + lon // 16, lat % 2


def placer():
    x, y, z, c = coords()
    way = 1 + 2 * c
    xs = [lax.rem(x + d * way, 4) for d in range(4)]
    ys = [lax.rem(y + d * way, 4) * 4 for d in range(4)]
    zs = [lax.rem(z + d * way, 4) for d in range(4)]
    inner = [lax.rem(v, 2) * 16 for v in zs]
    outer = [lax.div(v, 2) * 2 for v in zs]
    cores = [c, 1 - c]

    def place(dx, dy, dz, dc):
        return inner[dz] + ys[dy] + xs[dx], outer[dz] + cores[dc]

    return place


def to(lon, lat):
    return {"lon": lon, "lat": lat}


def iota(shape, dim):
    return lax.broadcasted_iota(jnp.int32, shape, dim)


def split(value):
    high = value.astype(jnp.bfloat16).astype(jnp.float32)
    return high, value - high


def lanes(low, high):
    lane = iota((1, LANES), 1)
    return (lane == low) | (lane == high)


def pack_ends(i, value, field):
    return jnp.where(lanes(2 * i, 2 * i + 1), pltpu.roll(value, 2 * i + 1, 1), field)


def pack_near(i, value, field):
    return jnp.where(lanes(2 * i, 2 * i + 3), pltpu.roll(value, 2 * i + 2, 1), field)


def put_ends(i, field, value):
    ends = pltpu.roll(field, LANES - 1 - 2 * i, 1)
    return jnp.where(lanes(LANES - 1, 0), ends, value)


def spread_ends(field):
    even = lax.rem(iota((1, LANES), 1), 2) == 0
    return jnp.where(even, field, pltpu.roll(field, 2, 1))


def transport(x, east, west, north, south, a, b):
    along = jnp.where(a > 0, east, west)
    over = jnp.where(b > 0, north, south)
    return x + jnp.abs(a) * (along - x) + jnp.abs(b) * (over - x)


def convect(columns, mixer):
    sources, inside = [], []
    for field, top, strength in columns:
        inner = iota((LEV, LANES), 0) < top
        source = jnp.where(inner, field * strength, 0.0)
        pad = jnp.zeros((DEPTH - LEV, LANES), jnp.float32)
        source = jnp.concatenate([source, pad], axis=0)
        high = source.astype(jnp.bfloat16)
        rest = (source - high.astype(jnp.float32)).astype(jnp.bfloat16)
        sources.append(jnp.concatenate([high, rest, high], axis=0))
        inside.append(inner)
    stack = jnp.concatenate(sources, axis=1)
    mixed = jnp.dot(mixer, stack, preferred_element_type=jnp.float32)
    return [
        column[0] + jnp.where(inner, mixed[:, h * LANES : (h + 1) * LANES], 0.0)
        for h, (column, inner) in enumerate(zip(columns, inside))
    ]


def kernel(
    kernels,
    residuals_in,
    columns_in,
    counts_in,
    courant,
    strength_in,
    cloud_top_in,
    redistribution_in,
    out,
    out_ends,
    flux,
    flux_ends,
    residuals,
    columns,
    counts,
    strength,
    cloud_top,
    redistribution,
    small_sem,
    forcing_in,
    wind,
    send,
    recv,
    state_0,
    state_1,
    state_2,
    state_3,
    edge,
    from_south,
    from_north,
    strip_wind,
    strip_strength,
    strip_top,
    mixer,
    spread,
    load_sem,
    wind_sem,
    send_sem,
    recv_sem,
    edge_send,
    edge_recv,
):
    states = (state_0, state_1, state_2, state_3)
    lon, lat = lax.axis_index("lon"), lax.axis_index("lat")
    core = lat % 2
    at_offset = placer()
    barrier = pltpu.get_barrier_semaphore()
    for offset in reversed(OFFSETS):
        for c in range(2):
            if any(offset) or c:
                pl.semaphore_signal(barrier, 1, device_id=to(*at_offset(*offset, c)))

    chips = [at_offset(*offset, 0) for offset in OFFSETS]
    chips = [there_lon * 2 + lax.div(there_lat, 2) for there_lon, there_lat in chips]

    def load(m):
        at = pl.ds(pl.multiple_of(chips[m] * LANES, LANES), LANES)
        return pltpu.make_async_copy(
            kernels.at[:, at], forcing_in.at[:, at], load_sem.at[m]
        )

    small = [
        pltpu.make_async_copy(source, target, small_sem.at[i])
        for i, (source, target) in enumerate(
            (
                (counts_in, counts),
                (residuals_in, residuals),
                (columns_in, columns),
                (strength_in, strength),
                (cloud_top_in, cloud_top),
                (redistribution_in, redistribution),
            )
        )
    ]
    for copy in small:
        copy.start()
    for m in range(CHIPS):
        load(m).start()
    def fetch(i, carry):
        for part in range(2):
            pltpu.make_async_copy(
                courant.at[part, :, i, :], wind.at[part, i], wind_sem
            ).start()
        return carry


    lane = iota((8, LANES), 1)
    sub = iota((8, LANES), 0)
    low = lane < 64

    def lo_half(shape):
        return iota(shape, 1) < 64

    def block_copy(k, there):
        return pltpu.make_async_remote_copy(
            src_ref=send.at[k],
            dst_ref=recv.at[k],
            send_sem=send_sem.at[k],
            recv_sem=recv_sem.at[k],
            device_id=to(*there),
        )

    mine = DEVICES - 2

    def send_to(m):
        load(m).wait()
        chip = chips[m]
        one = counts[0, 2 * chip]
        two = counts[0, 2 * chip + 1]
        row = iota((1, LANES), 1)
        live = (row % 64) < jnp.where(row < 64, one, two)
        weight = jnp.where(live, residuals[pl.ds(chip, 1), :], 0.0)
        place = columns[pl.ds(chip, 1), :].astype(jnp.float32)
        start = pl.multiple_of(chip * LANES, LANES)
        value = forcing_in[:, pl.ds(start, LANES)] * weight
        a, b, last = value[0:32], value[32:64], value[64:72]
        half = lo_half((32, LANES))
        turned = pltpu.roll(last, 4, 0)
        tail_0 = jnp.where(low, last, pltpu.roll(turned, 64, 1))
        tail_1 = jnp.where(low, pltpu.roll(last, 64, 1), turned)
        place_8 = jnp.broadcast_to(place, (8, LANES))
        tail_0 = jnp.where(sub == 4, place_8, tail_0)
        tail_1 = jnp.where(sub == 4, pltpu.roll(place_8, 64, 1), tail_1)
        slot_0 = 2 * m + core
        slot_1 = 2 * m + 1 - core
        send[slot_0, 0:32, :] = jnp.where(half, a, pltpu.roll(b, 64, 1))
        send[slot_1, 0:32, :] = jnp.where(half, pltpu.roll(a, 64, 1), b)
        send[slot_0, 32:ROWS, :] = tail_0[0:5]
        send[slot_1, 32:ROWS, :] = tail_1[0:5]
        for c in range(2):
            if 2 * m + c != mine:
                block_copy(2 * m + c, at_offset(*OFFSETS[m], c)).start()
            else:
                recv[mine] = send[mine]

    for copy in small:
        copy.wait()
    pl.semaphore_wait(barrier, DEVICES - 1)
    for m in range(CHIPS):
        send_to(m)
    lax.fori_loop(0, CLON, fetch, 0)

    high, rest = split(redistribution[...].T)
    pad = jnp.zeros((LEV, DEPTH - LEV), jnp.float32)
    mixer[...] = jnp.concatenate([high, pad, high, pad, rest, pad], axis=1).astype(
        jnp.bfloat16
    )

    def clear(i, carry):
        state_0[i] = jnp.zeros((LEV, LANES), jnp.float32)
        return carry

    lax.fori_loop(1, CLON + 1, clear, 0)

    pltpu.make_async_copy(wind, wind, wind_sem).wait()
    nothing = jnp.zeros((LEV, LANES), jnp.float32)
    few = jnp.zeros((8, LANES), jnp.float32)

    def pack_static(g, fields):
        a, b, c, d = fields
        for k in range(UNROLL):
            i = g * UNROLL + k
            a = pack_ends(i, wind[0, i], a)
            b = pack_ends(i, wind[1, i], b)
            row = strength[pl.ds(i, 1), :]
            c = pack_ends(i, jnp.broadcast_to(row, (8, LANES)), c)
            row = cloud_top[pl.ds(i, 1), :].astype(jnp.float32)
            d = pack_ends(i, jnp.broadcast_to(row, (8, LANES)), d)
        return a, b, c, d

    strips = lax.fori_loop(0, CLON // UNROLL, pack_static, (nothing, nothing, few, few))
    strip_wind[0], strip_wind[1], strip_strength[...] = strips[:3]
    strip_top[...] = strips[3].astype(jnp.int32)

    def paired(k):
        half = lo_half((32, LANES))
        one, two = recv[k, 0:32, :], recv[k + 1, 0:32, :]
        end_1, end_2 = recv[k, 29:ROWS, :], recv[k + 1, 29:ROWS, :]
        top = jnp.where(half, one, pltpu.roll(two, 64, 1))
        bottom = jnp.where(half, pltpu.roll(one, 64, 1), two)
        end_top = jnp.where(low, end_1, pltpu.roll(end_2, 64, 1))
        end_bottom = jnp.where(low, pltpu.roll(end_1, 64, 1), end_2)
        end = jnp.where(sub < 4, pltpu.roll(end_top, 5, 0), pltpu.roll(end_bottom, 1, 0))
        return jnp.concatenate([top, bottom, end], axis=0), end_top[7:8]

    east, west = lax.rem(lon + 1, 32), lax.rem(lon + 31, 32)
    north, south = lax.rem(lat + 1, 4), lax.rem(lat + 3, 4)

    def edge_copies(s, which=range(4)):
        parts = (
            (states[s].at[1], states[s].at[CLON + 1], (west, lat)),
            (states[s].at[CLON], states[s].at[0], (east, lat)),
            (edge.at[s], from_south.at[s], (lon, north)),
            (edge.at[s], from_north.at[s], (lon, south)),
        )
        return [
            pltpu.make_async_remote_copy(
                src_ref=source,
                dst_ref=target,
                send_sem=edge_send.at[4 * s + i],
                recv_sem=edge_recv.at[4 * s + i],
                device_id=to(*there),
            )
            for i, (source, target, there) in enumerate(parts)
            if i in which
        ]

    order = [0, CLON // 2 - 1, *range(1, CLON // 2 - 1)]

    def gather(first, blocks):
        values, places = [], []
        for i in range(blocks):
            if not isinstance(first, int) or first + i != mine:
                block_copy(first + i, (lon, lat)).wait_recv()
        for i in range(0, blocks, 2):
            value, place = paired(first + i)
            high, rest = split(value)
            values.append(jnp.concatenate([high, rest], axis=0))
            places.append(place)
        both = jnp.concatenate(values, axis=1).astype(jnp.bfloat16)
        place = jnp.concatenate(places, axis=1).astype(jnp.int32)
        across = lax.div(place, 256)
        within = lax.rem(place, 256)
        hot = iota((256, blocks * 64), 0) == within
        hot = jnp.where(hot, 1.0, 0.0).astype(jnp.bfloat16)
        for pairs in zip(order[::2], order[1::2]):
            masks = [
                jnp.where(across == q, 1.0, 0.0).astype(jnp.bfloat16) for q in pairs
            ]
            put = lax.dot_general(
                jnp.concatenate([both * mask for mask in masks], axis=0),
                hot,
                (((1,), (1,)), ((), ())),
                preferred_element_type=jnp.float32,
            )
            for h, q in enumerate(pairs):
                part = put[2 * h * LEV : (2 * h + 1) * LEV]
                part = part + put[(2 * h + 1) * LEV : (2 * h + 2) * LEV]
                state_0[2 * q + 1] += part[:, :LANES]
                state_0[2 * q + 2] += part[:, LANES:]
            if pairs[0] == 0 and isinstance(first, int) and first + blocks == DEVICES:
                for copy in edge_copies(0, range(2)):
                    copy.start()

    def gather_step(t, carry):
        gather(BLOCKS * t, BLOCKS)
        return carry

    lax.fori_loop(0, DEVICES // BLOCKS - 1, gather_step, 0)
    for first in range(DEVICES - BLOCKS, DEVICES, LAST):
        gather(first, LAST)

    def pack_first(g, fields):
        ends, near = fields
        for k in range(UNROLL):
            i = g * UNROLL + k
            value = state_0[i + 1]
            ends, near = pack_ends(i, value, ends), pack_near(i, value, near)
        return ends, near

    first = lax.fori_loop(0, CLON // UNROLL, pack_first, (nothing, nothing))
    edge[0], near = first
    for copy in edge_copies(0, range(2, 4)):
        copy.start()
    flux[...] = jnp.zeros((CLON, LANES), jnp.float32)
    flux_ends[...] = few

    lane_row = iota((1, LANES), 1)
    even = lax.rem(lane_row, 2) == 0

    for s in range(STEPS):
        now = states[s]
        last = s + 1 == STEPS
        later = out if last else states[s + 1]
        shift = 0 if last else 1

        def row(i, halos=None):
            x, west, east = now[i + 1], now[i], now[i + 2]
            after, before = pltpu.roll(x, LANES - 1, 1), pltpu.roll(x, 1, 1)
            if halos:
                above, below = halos
                if i:
                    west = put_ends(i - 1, edge[s], west)
                else:
                    east = put_ends(i + 1, edge[s], east)
                above = pltpu.roll(above, LANES - 2 - 2 * i, 1)
                below = pltpu.roll(below, (LANES - 2 * i) % LANES, 1)
                after = jnp.where(lane_row == LANES - 1, above, after)
                before = jnp.where(lane_row == 0, below, before)
            elif s:
                ends = pltpu.roll(spread[...], LANES - 2 - 2 * i, 1)
                after = jnp.where(lane_row == LANES - 2, ends, after)
                before = jnp.where(lane_row == 1, ends, before)
            moved = transport(x, east, west, after, before, wind[0, i], wind[1, i])
            return moved, cloud_top[pl.ds(i, 1), :], strength[pl.ds(i, 1), :]

        def advance_pair(i, field):
            values = convect([row(i), row(i + 1)], mixer[...])
            for h, value in enumerate(values):
                later[i + h + shift] = value
                flux[pl.ds(i + h, 1), :] += value[0:1]
                if not last:
                    field = pack_near(i + h, value, field)
            return field

        def advance(g, field):
            for k in range(PAIRS):
                field = advance_pair(1 + 2 * (g * PAIRS + k), field)
            return field

        groups = (CLON - 2) // 2 // PAIRS
        next_near = lax.fori_loop(0, groups, advance, nothing)
        for i in range(1 + 2 * groups * PAIRS, CLON - 1, 2):
            next_near = advance_pair(i, next_near)

        x = edge[s]
        near = jnp.where(even, near, pltpu.roll(near, LANES - 2, 1))
        east_of, west_of = pltpu.roll(x, LANES - 2, 1), pltpu.roll(x, 2, 1)
        for copy in edge_copies(s):
            copy.wait_recv()
        above = jnp.where(lat < 3, from_north[s], 0.0)
        below = jnp.where(lat > 0, from_south[s], 0.0)
        borders = (0, CLON - 1)
        values = convect([row(i, (above, below)) for i in borders], mixer[...])
        for i, value in zip(borders, values):
            later[i + shift] = value
        if not last:
            for copy in edge_copies(s + 1, range(2)):
                copy.start()
        moved = transport(
            x,
            pack_ends(CLON - 1, now[CLON + 1], east_of),
            pack_ends(0, now[0], west_of),
            jnp.where(even, pltpu.roll(above, LANES - 1, 1), near),
            jnp.where(even, near, pltpu.roll(below, 1, 1)),
            strip_wind[0],
            strip_wind[1],
        )
        strip = (moved, strip_top[0:1, :], strip_strength[0:1, :])
        (ends,) = convect([strip], mixer[...])
        flux_ends[...] += ends[0:8]
        if last:
            out_ends[...] = ends
        else:
            edge[s + 1] = ends
            for copy in edge_copies(s + 1, range(2, 4)):
                copy.start()
            spread[...] = spread_ends(ends)
        for i, value in zip(borders, values):
            flux[pl.ds(i, 1), :] += value[0:1]
            if not last:
                next_near = pack_near(i, value, next_near)
        near = next_near

    def sent(k, carry):
        block_copy(k, (lon, lat)).wait_send()
        return carry

    lax.fori_loop(0, mine, sent, 0)
    block_copy(DEVICES - 1, (lon, lat)).wait_send()
    for s in range(STEPS):
        for copy in edge_copies(s):
            copy.wait_send()


def finish(field, ends, flux_in, flux_ends, out, flux, whole, whole_flux, sem, flux_sem):
    def group(g, carry):
        for k in range(UNROLL):
            i = g * UNROLL + k
            whole[i] = put_ends(i, ends[...], field[i])
            pltpu.make_async_copy(whole.at[i], out.at[:, i, :], sem).start()
            total = jnp.broadcast_to(flux_in[pl.ds(i, 1), :], (8, LANES))
            whole_flux[pl.ds(i, 1), :] = put_ends(i, flux_ends[...], total)[0:1]
        return carry

    lax.fori_loop(0, CLON // UNROLL, group, 0)
    last = pltpu.make_async_copy(whole_flux, flux, flux_sem)
    last.start()
    pltpu.make_async_copy(out, out, sem).wait()
    last.wait()


def on_device(
    kernels,
    weighted_residuals,
    sounding_columns,
    segment_counts,
    courant,
    mix_strength,
    cloud_top,
    redistribution,
):
    in_vmem = pl.BlockSpec(memory_space=pltpu.VMEM)
    f32 = jnp.float32
    parts = pl.pallas_call(
        kernel,
        out_shape=(
            pltpu.VMEM((CLON, LEV, LANES), f32),
            pltpu.VMEM((LEV, LANES), f32),
            pltpu.VMEM((CLON, LANES), f32),
            pltpu.VMEM((8, LANES), f32),
        ),
        in_specs=[pl.BlockSpec(memory_space=pl.ANY)] * 8,
        out_specs=(in_vmem,) * 4,
        scratch_shapes=[
            pltpu.VMEM((CHIPS, LANES), f32),
            pltpu.VMEM((CHIPS, LANES), jnp.int32),
            pltpu.SMEM((1, DEVICES), jnp.int32),
            pltpu.VMEM((CLON, LANES), f32),
            pltpu.VMEM((CLON, LANES), jnp.int32),
            pltpu.VMEM((LEV, LEV), f32),
            pltpu.SemaphoreType.DMA((6,)),
            pltpu.VMEM((LEV, CHIPS * LANES), f32),
            pltpu.VMEM((2, CLON, LEV, LANES), f32),
            pltpu.VMEM((DEVICES, ROWS, LANES), f32),
            pltpu.VMEM((DEVICES, ROWS, LANES), f32),
            *[pltpu.VMEM((CLON + 2, LEV, LANES), f32) for _ in range(STEPS)],
            pltpu.VMEM((STEPS, LEV, LANES), f32),
            pltpu.VMEM((STEPS, LEV, LANES), f32),
            pltpu.VMEM((STEPS, LEV, LANES), f32),
            pltpu.VMEM((2, LEV, LANES), f32),
            pltpu.VMEM((8, LANES), f32),
            pltpu.VMEM((8, LANES), jnp.int32),
            pltpu.VMEM((LEV, 3 * DEPTH), jnp.bfloat16),
            pltpu.VMEM((LEV, LANES), f32),
            pltpu.SemaphoreType.DMA((CHIPS,)),
            pltpu.SemaphoreType.DMA,
            pltpu.SemaphoreType.DMA((DEVICES,)),
            pltpu.SemaphoreType.DMA((DEVICES,)),
            pltpu.SemaphoreType.DMA((4 * STEPS,)),
            pltpu.SemaphoreType.DMA((4 * STEPS,)),
        ],
        compiler_params=pltpu.CompilerParams(
            collective_id=0, has_side_effects=True, vmem_limit_bytes=44 * 2**20
        ),
    )(
        *(
            pltpu.with_memory_space_constraint(value, pltpu.HBM)
            for value in (
                kernels,
                weighted_residuals.reshape(CHIPS, LANES),
                sounding_columns.reshape(CHIPS, LANES),
                segment_counts,
                courant,
                mix_strength,
                cloud_top,
                redistribution,
            )
        )
    )
    return pl.pallas_call(
        finish,
        out_shape=(
            jax.ShapeDtypeStruct((LEV, CLON, LANES), f32),
            jax.ShapeDtypeStruct((CLON, LANES), f32),
        ),
        in_specs=[in_vmem] * 4,
        out_specs=(pl.BlockSpec(memory_space=pl.ANY),) * 2,
        scratch_shapes=[
            pltpu.VMEM((CLON, LEV, LANES), f32),
            pltpu.VMEM((CLON, LANES), f32),
            pltpu.SemaphoreType.DMA,
            pltpu.SemaphoreType.DMA,
        ],
        compiler_params=pltpu.CompilerParams(vmem_limit_bytes=16 * 2**20),
    )(*parts)


def solution(mesh):
    return jax.shard_map(
        on_device,
        mesh=mesh,
        in_specs=(
            P(None, ("lon", "lat")),
            P(("lon", "lat")),
            P(("lon", "lat")),
            P(("lon", "lat"), None),
            P(None, None, "lon", "lat"),
            P("lon", "lat"),
            P("lon", "lat"),
            P(),
        ),
        out_specs=(P(None, "lon", "lat"), P("lon", "lat")),
        check_vma=False,
    )
```

```python
import itertools
import random

import jax
import jax.numpy as jnp
from jax import lax
from jax.experimental import pallas as pl
from jax.experimental.pallas import tpu as pltpu
from jax.sharding import PartitionSpec as P

STEPS = 4
LEV = 72
CLON = 48
LANES = 128
CHIPS = 64
DEVICES = 128
ROWS = 37
BLOCKS = 8
UNROLL = 12
PAIRS = 11
LAST = 8
DEPTH = 80

OFFSETS = list(itertools.product(range(4), repeat=3))
random.Random(1).shuffle(OFFSETS)
JITTER = random.Random(1)
OFFSETS.sort(key=lambda o: sum(min(v, 4 - v) for v in o) + JITTER.random() * 1.5)
OFFSETS.remove((0, 0, 0))
OFFSETS.append((0, 0, 0))


def coords():
    lon = lax.axis_index("lon")
    lat = lax.axis_index("lat")
    return lon % 4, (lon // 4) % 4, (lat // 2) * 2 + lon // 16, lat % 2


def placer():
    x, y, z, c = coords()
    way = 1 + 2 * c
    xs = [lax.rem(x + d * way, 4) for d in range(4)]
    ys = [lax.rem(y + d * way, 4) * 4 for d in range(4)]
    zs = [lax.rem(z + d * way, 4) for d in range(4)]
    inner = [lax.rem(v, 2) * 16 for v in zs]
    outer = [lax.div(v, 2) * 2 for v in zs]
    cores = [c, 1 - c]

    def place(dx, dy, dz, dc):
        return inner[dz] + ys[dy] + xs[dx], outer[dz] + cores[dc]

    return place


def to(lon, lat):
    return {"lon": lon, "lat": lat}


def iota(shape, dim):
    return lax.broadcasted_iota(jnp.int32, shape, dim)


def split(value):
    high = value.astype(jnp.bfloat16).astype(jnp.float32)
    return high, value - high


def lanes(low, high):
    lane = iota((1, LANES), 1)
    return (lane == low) | (lane == high)


def pack_ends(i, value, field):
    return jnp.where(lanes(2 * i, 2 * i + 1), pltpu.roll(value, 2 * i + 1, 1), field)


def pack_near(i, value, field):
    return jnp.where(lanes(2 * i, 2 * i + 3), pltpu.roll(value, 2 * i + 2, 1), field)


def put_ends(i, field, value):
    ends = pltpu.roll(field, LANES - 1 - 2 * i, 1)
    return jnp.where(lanes(LANES - 1, 0), ends, value)


def spread_ends(field):
    even = lax.rem(iota((1, LANES), 1), 2) == 0
    return jnp.where(even, field, pltpu.roll(field, 2, 1))


def transport(x, east, west, north, south, a, b):
    along = jnp.where(a > 0, east, west)
    over = jnp.where(b > 0, north, south)
    return x + jnp.abs(a) * (along - x) + jnp.abs(b) * (over - x)


def convect(columns, mixer):
    sources, inside = [], []
    for field, top, strength in columns:
        inner = iota((LEV, LANES), 0) < top
        source = jnp.where(inner, field * strength, 0.0)
        pad = jnp.zeros((DEPTH - LEV, LANES), jnp.float32)
        source = jnp.concatenate([source, pad], axis=0)
        high = source.astype(jnp.bfloat16)
        rest = (source - high.astype(jnp.float32)).astype(jnp.bfloat16)
        sources.append(jnp.concatenate([high, rest, high], axis=0))
        inside.append(inner)
    stack = jnp.concatenate(sources, axis=1)
    mixed = jnp.dot(mixer, stack, preferred_element_type=jnp.float32)
    return [
        column[0] + jnp.where(inner, mixed[:, h * LANES : (h + 1) * LANES], 0.0)
        for h, (column, inner) in enumerate(zip(columns, inside))
    ]


def kernel(
    kernels,
    residuals_in,
    columns_in,
    counts_in,
    courant,
    strength_in,
    cloud_top_in,
    redistribution_in,
    out,
    out_ends,
    flux,
    flux_ends,
    residuals,
    columns,
    counts,
    strength,
    cloud_top,
    redistribution,
    small_sem,
    forcing_in,
    wind,
    send,
    recv,
    state_0,
    state_1,
    state_2,
    state_3,
    edge,
    from_south,
    from_north,
    strip_wind,
    strip_strength,
    strip_top,
    mixer,
    spread,
    load_sem,
    wind_sem,
    send_sem,
    recv_sem,
    edge_send,
    edge_recv,
):
    states = (state_0, state_1, state_2, state_3)
    lon, lat = lax.axis_index("lon"), lax.axis_index("lat")
    core = lat % 2
    at_offset = placer()
    barrier = pltpu.get_barrier_semaphore()
    for offset in reversed(OFFSETS):
        for c in range(2):
            if any(offset) or c:
                pl.semaphore_signal(barrier, 1, device_id=to(*at_offset(*offset, c)))

    chips = [at_offset(*offset, 0) for offset in OFFSETS]
    chips = [there_lon * 2 + lax.div(there_lat, 2) for there_lon, there_lat in chips]

    def load(m):
        at = pl.ds(pl.multiple_of(chips[m] * LANES, LANES), LANES)
        return pltpu.make_async_copy(
            kernels.at[:, at], forcing_in.at[:, at], load_sem.at[m]
        )

    small = [
        pltpu.make_async_copy(source, target, small_sem.at[i])
        for i, (source, target) in enumerate(
            (
                (counts_in, counts),
                (residuals_in, residuals),
                (columns_in, columns),
                (strength_in, strength),
                (cloud_top_in, cloud_top),
                (redistribution_in, redistribution),
            )
        )
    ]
    for copy in small:
        copy.start()
    for m in range(CHIPS):
        load(m).start()
    def fetch(i, carry):
        for part in range(2):
            pltpu.make_async_copy(
                courant.at[part, :, i, :], wind.at[part, i], wind_sem
            ).start()
        return carry


    lane = iota((8, LANES), 1)
    sub = iota((8, LANES), 0)
    low = lane < 64

    def lo_half(shape):
        return iota(shape, 1) < 64

    def block_copy(k, there):
        return pltpu.make_async_remote_copy(
            src_ref=send.at[k],
            dst_ref=recv.at[k],
            send_sem=send_sem.at[k],
            recv_sem=recv_sem.at[k],
            device_id=to(*there),
        )

    mine = DEVICES - 2

    def send_to(m):
        load(m).wait()
        chip = chips[m]
        one = counts[0, 2 * chip]
        two = counts[0, 2 * chip + 1]
        row = iota((1, LANES), 1)
        live = (row % 64) < jnp.where(row < 64, one, two)
        weight = jnp.where(live, residuals[pl.ds(chip, 1), :], 0.0)
        place = columns[pl.ds(chip, 1), :].astype(jnp.float32)
        start = pl.multiple_of(chip * LANES, LANES)
        value = forcing_in[:, pl.ds(start, LANES)] * weight
        a, b, last = value[0:32], value[32:64], value[64:72]
        half = lo_half((32, LANES))
        turned = pltpu.roll(last, 4, 0)
        tail_0 = jnp.where(low, last, pltpu.roll(turned, 64, 1))
        tail_1 = jnp.where(low, pltpu.roll(last, 64, 1), turned)
        place_8 = jnp.broadcast_to(place, (8, LANES))
        tail_0 = jnp.where(sub == 4, place_8, tail_0)
        tail_1 = jnp.where(sub == 4, pltpu.roll(place_8, 64, 1), tail_1)
        slot_0 = 2 * m + core
        slot_1 = 2 * m + 1 - core
        send[slot_0, 0:32, :] = jnp.where(half, a, pltpu.roll(b, 64, 1))
        send[slot_1, 0:32, :] = jnp.where(half, pltpu.roll(a, 64, 1), b)
        send[slot_0, 32:ROWS, :] = tail_0[0:5]
        send[slot_1, 32:ROWS, :] = tail_1[0:5]
        for c in range(2):
            if 2 * m + c != mine:
                block_copy(2 * m + c, at_offset(*OFFSETS[m], c)).start()
            else:
                recv[mine] = send[mine]

    for copy in small:
        copy.wait()
    pl.semaphore_wait(barrier, DEVICES - 1)
    for m in range(CHIPS):
        send_to(m)
    lax.fori_loop(0, CLON, fetch, 0)

    high, rest = split(redistribution[...].T)
    pad = jnp.zeros((LEV, DEPTH - LEV), jnp.float32)
    mixer[...] = jnp.concatenate([high, pad, high, pad, rest, pad], axis=1).astype(
        jnp.bfloat16
    )

    def clear(i, carry):
        state_0[i] = jnp.zeros((LEV, LANES), jnp.float32)
        return carry

    lax.fori_loop(1, CLON + 1, clear, 0)

    pltpu.make_async_copy(wind, wind, wind_sem).wait()
    nothing = jnp.zeros((LEV, LANES), jnp.float32)
    few = jnp.zeros((8, LANES), jnp.float32)

    def pack_static(g, fields):
        a, b, c, d = fields
        for k in range(UNROLL):
            i = g * UNROLL + k
            a = pack_ends(i, wind[0, i], a)
            b = pack_ends(i, wind[1, i], b)
            row = strength[pl.ds(i, 1), :]
            c = pack_ends(i, jnp.broadcast_to(row, (8, LANES)), c)
            row = cloud_top[pl.ds(i, 1), :].astype(jnp.float32)
            d = pack_ends(i, jnp.broadcast_to(row, (8, LANES)), d)
        return a, b, c, d

    strips = lax.fori_loop(0, CLON // UNROLL, pack_static, (nothing, nothing, few, few))
    strip_wind[0], strip_wind[1], strip_strength[...] = strips[:3]
    strip_top[...] = strips[3].astype(jnp.int32)

    def paired(k):
        half = lo_half((32, LANES))
        one, two = recv[k, 0:32, :], recv[k + 1, 0:32, :]
        end_1, end_2 = recv[k, 29:ROWS, :], recv[k + 1, 29:ROWS, :]
        top = jnp.where(half, one, pltpu.roll(two, 64, 1))
        bottom = jnp.where(half, pltpu.roll(one, 64, 1), two)
        end_top = jnp.where(low, end_1, pltpu.roll(end_2, 64, 1))
        end_bottom = jnp.where(low, pltpu.roll(end_1, 64, 1), end_2)
        end = jnp.where(sub < 4, pltpu.roll(end_top, 5, 0), pltpu.roll(end_bottom, 1, 0))
        return jnp.concatenate([top, bottom, end], axis=0), end_top[7:8]

    east, west = lax.rem(lon + 1, 32), lax.rem(lon + 31, 32)
    north, south = lax.rem(lat + 1, 4), lax.rem(lat + 3, 4)

    def edge_copies(s, which=range(4)):
        parts = (
            (states[s].at[1], states[s].at[CLON + 1], (west, lat)),
            (states[s].at[CLON], states[s].at[0], (east, lat)),
            (edge.at[s], from_south.at[s], (lon, north)),
            (edge.at[s], from_north.at[s], (lon, south)),
        )
        return [
            pltpu.make_async_remote_copy(
                src_ref=source,
                dst_ref=target,
                send_sem=edge_send.at[4 * s + i],
                recv_sem=edge_recv.at[4 * s + i],
                device_id=to(*there),
            )
            for i, (source, target, there) in enumerate(parts)
            if i in which
        ]

    order = [0, CLON // 2 - 1, *range(1, CLON // 2 - 1)]

    def gather(first, blocks):
        values, places = [], []
        for i in range(blocks):
            if not isinstance(first, int) or first + i != mine:
                block_copy(first + i, (lon, lat)).wait_recv()
        for i in range(0, blocks, 2):
            value, place = paired(first + i)
            high, rest = split(value)
            values.append(jnp.concatenate([high, rest], axis=0))
            places.append(place)
        both = jnp.concatenate(values, axis=1).astype(jnp.bfloat16)
        place = jnp.concatenate(places, axis=1).astype(jnp.int32)
        across = lax.div(place, 256)
        within = lax.rem(place, 256)
        hot = iota((256, blocks * 64), 0) == within
        hot = jnp.where(hot, 1.0, 0.0).astype(jnp.bfloat16)
        for pairs in zip(order[::2], order[1::2]):
            masks = [
                jnp.where(across == q, 1.0, 0.0).astype(jnp.bfloat16) for q in pairs
            ]
            put = lax.dot_general(
                jnp.concatenate([both * mask for mask in masks], axis=0),
                hot,
                (((1,), (1,)), ((), ())),
                preferred_element_type=jnp.float32,
            )
            for h, q in enumerate(pairs):
                part = put[2 * h * LEV : (2 * h + 1) * LEV]
                part = part + put[(2 * h + 1) * LEV : (2 * h + 2) * LEV]
                state_0[2 * q + 1] += part[:, :LANES]
                state_0[2 * q + 2] += part[:, LANES:]
            if pairs[0] == 0 and isinstance(first, int) and first + blocks == DEVICES:
                for copy in edge_copies(0, range(2)):
                    copy.start()

    def gather_step(t, carry):
        gather(BLOCKS * t, BLOCKS)
        return carry

    lax.fori_loop(0, DEVICES // BLOCKS - 1, gather_step, 0)
    for first in range(DEVICES - BLOCKS, DEVICES, LAST):
        gather(first, LAST)

    def pack_first(g, fields):
        ends, near = fields
        for k in range(UNROLL):
            i = g * UNROLL + k
            value = state_0[i + 1]
            ends, near = pack_ends(i, value, ends), pack_near(i, value, near)
        return ends, near

    first = lax.fori_loop(0, CLON // UNROLL, pack_first, (nothing, nothing))
    edge[0], near = first
    for copy in edge_copies(0, range(2, 4)):
        copy.start()
    flux[...] = jnp.zeros((CLON, LANES), jnp.float32)
    flux_ends[...] = few

    lane_row = iota((1, LANES), 1)
    even = lax.rem(lane_row, 2) == 0

    def sent(k, carry):
        block_copy(k, (lon, lat)).wait_send()
        return carry

    for s in range(STEPS):
        now = states[s]
        last = s + 1 == STEPS
        later = out if last else states[s + 1]
        shift = 0 if last else 1

        def row(i, halos=None):
            x, west, east = now[i + 1], now[i], now[i + 2]
            after, before = pltpu.roll(x, LANES - 1, 1), pltpu.roll(x, 1, 1)
            if halos:
                above, below = halos
                if i:
                    west = put_ends(i - 1, edge[s], west)
                else:
                    east = put_ends(i + 1, edge[s], east)
                above = pltpu.roll(above, LANES - 2 - 2 * i, 1)
                below = pltpu.roll(below, (LANES - 2 * i) % LANES, 1)
                after = jnp.where(lane_row == LANES - 1, above, after)
                before = jnp.where(lane_row == 0, below, before)
            elif s:
                ends = pltpu.roll(spread[...], LANES - 2 - 2 * i, 1)
                after = jnp.where(lane_row == LANES - 2, ends, after)
                before = jnp.where(lane_row == 1, ends, before)
            moved = transport(x, east, west, after, before, wind[0, i], wind[1, i])
            return moved, cloud_top[pl.ds(i, 1), :], strength[pl.ds(i, 1), :]

        def advance_pair(i, field):
            values = convect([row(i), row(i + 1)], mixer[...])
            for h, value in enumerate(values):
                later[i + h + shift] = value
                flux[pl.ds(i + h, 1), :] += value[0:1]
                if not last:
                    field = pack_near(i + h, value, field)
            return field

        def advance(g, field):
            for k in range(PAIRS):
                field = advance_pair(1 + 2 * (g * PAIRS + k), field)
            return field

        groups = (CLON - 2) // 2 // PAIRS
        next_near = lax.fori_loop(0, groups, advance, nothing)
        for i in range(1 + 2 * groups * PAIRS, CLON - 1, 2):
            next_near = advance_pair(i, next_near)

        share = DEVICES // STEPS
        lax.fori_loop(share * s, min(share * (s + 1), mine), sent, 0)
        if last:
            block_copy(DEVICES - 1, (lon, lat)).wait_send()
        if s:
            for copy in edge_copies(s - 1):
                copy.wait_send()

        x = edge[s]
        near = jnp.where(even, near, pltpu.roll(near, LANES - 2, 1))
        east_of, west_of = pltpu.roll(x, LANES - 2, 1), pltpu.roll(x, 2, 1)
        for copy in edge_copies(s):
            copy.wait_recv()
        above = jnp.where(lat < 3, from_north[s], 0.0)
        below = jnp.where(lat > 0, from_south[s], 0.0)
        borders = (0, CLON - 1)
        values = convect([row(i, (above, below)) for i in borders], mixer[...])
        for i, value in zip(borders, values):
            later[i + shift] = value
        if not last:
            for copy in edge_copies(s + 1, range(2)):
                copy.start()
        moved = transport(
            x,
            pack_ends(CLON - 1, now[CLON + 1], east_of),
            pack_ends(0, now[0], west_of),
            jnp.where(even, pltpu.roll(above, LANES - 1, 1), near),
            jnp.where(even, near, pltpu.roll(below, 1, 1)),
            strip_wind[0],
            strip_wind[1],
        )
        strip = (moved, strip_top[0:1, :], strip_strength[0:1, :])
        (ends,) = convect([strip], mixer[...])
        flux_ends[...] += ends[0:8]
        if last:
            out_ends[...] = ends
        else:
            edge[s + 1] = ends
            for copy in edge_copies(s + 1, range(2, 4)):
                copy.start()
            spread[...] = spread_ends(ends)
        for i, value in zip(borders, values):
            flux[pl.ds(i, 1), :] += value[0:1]
            if not last:
                next_near = pack_near(i, value, next_near)
        near = next_near

    for copy in edge_copies(STEPS - 1):
        copy.wait_send()


def finish(field, ends, flux_in, flux_ends, out, flux, whole, whole_flux, sem, flux_sem):
    def group(g, carry):
        for k in range(UNROLL):
            i = g * UNROLL + k
            whole[i] = put_ends(i, ends[...], field[i])
            pltpu.make_async_copy(whole.at[i], out.at[:, i, :], sem).start()
            total = jnp.broadcast_to(flux_in[pl.ds(i, 1), :], (8, LANES))
            whole_flux[pl.ds(i, 1), :] = put_ends(i, flux_ends[...], total)[0:1]
        return carry

    lax.fori_loop(0, CLON // UNROLL, group, 0)
    last = pltpu.make_async_copy(whole_flux, flux, flux_sem)
    last.start()
    pltpu.make_async_copy(out, out, sem).wait()
    last.wait()


def on_device(
    kernels,
    weighted_residuals,
    sounding_columns,
    segment_counts,
    courant,
    mix_strength,
    cloud_top,
    redistribution,
):
    in_vmem = pl.BlockSpec(memory_space=pltpu.VMEM)
    f32 = jnp.float32
    parts = pl.pallas_call(
        kernel,
        out_shape=(
            pltpu.VMEM((CLON, LEV, LANES), f32),
            pltpu.VMEM((LEV, LANES), f32),
            pltpu.VMEM((CLON, LANES), f32),
            pltpu.VMEM((8, LANES), f32),
        ),
        in_specs=[pl.BlockSpec(memory_space=pl.ANY)] * 8,
        out_specs=(in_vmem,) * 4,
        scratch_shapes=[
            pltpu.VMEM((CHIPS, LANES), f32),
            pltpu.VMEM((CHIPS, LANES), jnp.int32),
            pltpu.SMEM((1, DEVICES), jnp.int32),
            pltpu.VMEM((CLON, LANES), f32),
            pltpu.VMEM((CLON, LANES), jnp.int32),
            pltpu.VMEM((LEV, LEV), f32),
            pltpu.SemaphoreType.DMA((6,)),
            pltpu.VMEM((LEV, CHIPS * LANES), f32),
            pltpu.VMEM((2, CLON, LEV, LANES), f32),
            pltpu.VMEM((DEVICES, ROWS, LANES), f32),
            pltpu.VMEM((DEVICES, ROWS, LANES), f32),
            *[pltpu.VMEM((CLON + 2, LEV, LANES), f32) for _ in range(STEPS)],
            pltpu.VMEM((STEPS, LEV, LANES), f32),
            pltpu.VMEM((STEPS, LEV, LANES), f32),
            pltpu.VMEM((STEPS, LEV, LANES), f32),
            pltpu.VMEM((2, LEV, LANES), f32),
            pltpu.VMEM((8, LANES), f32),
            pltpu.VMEM((8, LANES), jnp.int32),
            pltpu.VMEM((LEV, 3 * DEPTH), jnp.bfloat16),
            pltpu.VMEM((LEV, LANES), f32),
            pltpu.SemaphoreType.DMA((CHIPS,)),
            pltpu.SemaphoreType.DMA,
            pltpu.SemaphoreType.DMA((DEVICES,)),
            pltpu.SemaphoreType.DMA((DEVICES,)),
            pltpu.SemaphoreType.DMA((4 * STEPS,)),
            pltpu.SemaphoreType.DMA((4 * STEPS,)),
        ],
        compiler_params=pltpu.CompilerParams(
            collective_id=0, has_side_effects=True, vmem_limit_bytes=44 * 2**20
        ),
    )(
        *(
            pltpu.with_memory_space_constraint(value, pltpu.HBM)
            for value in (
                kernels,
                weighted_residuals.reshape(CHIPS, LANES),
                sounding_columns.reshape(CHIPS, LANES),
                segment_counts,
                courant,
                mix_strength,
                cloud_top,
                redistribution,
            )
        )
    )
    return pl.pallas_call(
        finish,
        out_shape=(
            jax.ShapeDtypeStruct((LEV, CLON, LANES), f32),
            jax.ShapeDtypeStruct((CLON, LANES), f32),
        ),
        in_specs=[in_vmem] * 4,
        out_specs=(pl.BlockSpec(memory_space=pl.ANY),) * 2,
        scratch_shapes=[
            pltpu.VMEM((CLON, LEV, LANES), f32),
            pltpu.VMEM((CLON, LANES), f32),
            pltpu.SemaphoreType.DMA,
            pltpu.SemaphoreType.DMA,
        ],
        compiler_params=pltpu.CompilerParams(vmem_limit_bytes=16 * 2**20),
    )(*parts)


def solution(mesh):
    return jax.shard_map(
        on_device,
        mesh=mesh,
        in_specs=(
            P(None, ("lon", "lat")),
            P(("lon", "lat")),
            P(("lon", "lat")),
            P(("lon", "lat"), None),
            P(None, None, "lon", "lat"),
            P("lon", "lat"),
            P("lon", "lat"),
            P(),
        ),
        out_specs=(P(None, "lon", "lat"), P("lon", "lat")),
        check_vma=False,
    )
```
